32 devices in a mesh: dp: 4 (over x, core), ulysses: 4 (over z), blk: 2 (over y).
Axes of the slice: x: 2, y: 2, z: 4, core: 2. Of those that a mesh axis runs over, the one named last changes fastest.
Arguments:
- tokens: bfloat16 [8, 512, 2048], P('dp', ('ulysses', 'blk')), may hold values from -6 to 6
- memory: bfloat16 [8, 512, 2048], P('dp', ('ulysses', 'blk')), may hold values from -6 to 6
- lengths: int32 [8, 8], P('dp'), may hold values from 1 to 480, as said below
- gain_attn: float32 [2048], replicated, may hold values from 0.5 to 1.5
- gain_memory: float32 [2048], replicated, may hold values from 0.5 to 1.5
- gain_ffn: float32 [2048], replicated, may hold values from 0.5 to 1.5
- w_query: bfloat16 [2048, 2048], P(('dp', 'ulysses', 'blk')), may hold values from -0.125 to 0.125
- w_key: bfloat16 [2048, 2048], P(('dp', 'ulysses', 'blk')), may hold values from -0.125 to 0.125
- w_value: bfloat16 [2048, 2048], P(('dp', 'ulysses', 'blk')), may hold values from -0.125 to 0.125
- w_out: bfloat16 [2048, 2048], P(('dp', 'ulysses', 'blk')), may hold values from -0.75 to 0.75
- w_gate: bfloat16 [2048, 5504], P(('dp', 'ulysses', 'blk')), may hold values from -0.125 to 0.125
- w_up: bfloat16 [2048, 5504], P(('dp', 'ulysses', 'blk')), may hold values from -0.125 to 0.125
- w_down: bfloat16 [2048, 5504], P(('dp', 'ulysses', 'blk')), may hold values from -0.078125 to 0.078125
- cotangent: bfloat16 [8, 512, 2048], P('dp', ('ulysses', 'blk')), may hold values from -6 to 6
Outputs:
- output: bfloat16 [8, 512, 2048], P('dp', ('ulysses', 'blk'))
- grad_tokens: bfloat16 [8, 512, 2048], P('dp', ('ulysses', 'blk'))
- grad_memory: bfloat16 [8, 512, 2048], P('dp', ('ulysses', 'blk'))
- grad_gain_attn: float32 [2048], P(('dp', 'ulysses', 'blk'))
- grad_gain_memory: float32 [2048], P(('dp', 'ulysses', 'blk'))
- grad_gain_ffn: float32 [2048], P(('dp', 'ulysses', 'blk'))
- grad_query: float32 [2048, 2048], P('dp', ('ulysses', 'blk'))
- grad_key: float32 [2048, 2048], P('dp', ('ulysses', 'blk'))
- grad_value: float32 [2048, 2048], P('dp', ('ulysses', 'blk'))
- grad_out: float32 [2048, 2048], P('dp', ('ulysses', 'blk'))
- grad_gate: float32 [2048, 5504], P('dp', ('ulysses', 'blk'))
- grad_up: float32 [2048, 5504], P('dp', ('ulysses', 'blk'))
- grad_down: float32 [2048, 5504], P('dp', ('ulysses', 'blk'))
The draws below stay inside these ranges and needn't reach their ends.
Inputs may be any that keep to these rules, and one draw needn't show every extreme that they name: Each row of lengths gives, in order, the lengths of the 8 documents packed at its start; they sum to less than 512, the rest of the row is padding, and every row has one document of the largest length.
All inputs are finite; a program needn't handle non-finite values.
Results may differ from the reference program's by a relative error of at most 0.018.
Values may be sent and summed in bfloat16 or wider, within the bound.
No kernel may reach another device: no remote copies, remote signals or barrier semaphores. Data moves between devices by JAX's collectives and lax.ppermute only.
A program may use at most 320 MiB of HBM per device.

```python
import jax
import jax.numpy as jnp
from jax import lax

D = 2048
H = 16
HD = 128
FF = 5504
TOK_ROW = 64
DOCS = 8
SEQ = 512
ROWS = 8


def draw_lengths(key, part):
    key = jax.random.fold_in(key, 7)
    subkeys = jax.random.split(key, 3)
    places = jnp.arange(DOCS, dtype=jnp.int32)[None, :]
    leading = jax.random.randint(subkeys[0], (ROWS, 1), 0, 4)
    before = jax.random.randint(subkeys[1], (ROWS, DOCS), 1, TOK_ROW // 16 + 1)
    trailing = jax.random.randint(subkeys[2], (ROWS, DOCS), 1, max(TOK_ROW // 32, 1) + 1)
    shorter = jnp.where(places < leading, before, trailing)
    longest = SEQ - TOK_ROW // 2
    return jnp.where(places == leading, longest, shorter).astype(jnp.int32)


def spiked(entries, own_key, source, target, parts, factor):
    owner, partner = [(jnp.arange(entries.shape[axis_at]) // (entries.shape[axis_at] // parts)).reshape([-1 if axis == axis_at else 1 for axis in range(entries.ndim)]) for axis_at in (source, target)]
    chosen = jax.random.permutation(own_key, parts)[partner]
    strong = (owner == chosen) | (owner == (partner + parts // 2) % parts)
    return jnp.where(strong, factor * entries, entries)


def block_scale(stream_key, shape, cuts, least, high):
    level = 1.0
    for dim, shards_of in cuts:
        draws = jax.random.uniform(jax.random.fold_in(jax.random.fold_in(stream_key, 6), dim), (shards_of,), jnp.float32, least / len(cuts), high / len(cuts))
        level = level * jnp.repeat(jnp.exp(draws), shape[dim] // shards_of).reshape((-1,) + (1,) * (len(shape) - 1 - dim))
    return level


def noise(own_key, shape, width, reach, cuts=(), kind=jnp.bfloat16):
    result = jax.random.normal(own_key, shape, jnp.float32) * width
    if len(cuts) > 0:
        result = block_scale(own_key, shape, cuts, -0.22, 0.18) * result
    return jnp.clip(result, min=-reach, max=reach).astype(kind)


def noise_with(stream_key, shape, spread, limit, cuts, heavy, held_as=jnp.bfloat16):
    entries = spread * jax.random.normal(stream_key, shape, jnp.float32)
    if cuts:
        entries = entries * block_scale(stream_key, shape, cuts, -0.22, 0.18)
    return jnp.clip(spiked(entries, jax.random.fold_in(stream_key, 3), *heavy), -limit, limit).astype(held_as)


def setup_inputs(seed: int = 0) -> dict:
    arg_keys = jax.random.split(jax.random.key(seed), 15)
    tokens = noise(arg_keys[0], (ROWS, SEQ, D), 1.0, 6.0, ((0, 4), (1, 8)))
    memory = noise(arg_keys[1], (ROWS, SEQ, D), 1.0, 6.0, ((0, 4), (1, 8)))
    lengths = draw_lengths(jax.random.fold_in(arg_keys[14], 71), 0)
    gain_attn = jnp.clip(1.0 + 0.1 * jax.random.normal(arg_keys[3], (D,), jnp.float32), 0.5, 1.5)
    gain_memory = jnp.clip(1.0 + 0.1 * jax.random.normal(arg_keys[4], (D,), jnp.float32), 0.5, 1.5)
    gain_ffn = jnp.clip(1.0 + 0.1 * jax.random.normal(arg_keys[5], (D,), jnp.float32), 0.5, 1.5)
    w_query = noise(arg_keys[6], (D, H * HD), D ** -0.5, 0.125, ((0, 32),))
    w_key = noise(arg_keys[7], (D, H * HD), D ** -0.5, 0.125, ((0, 32),))
    w_value = noise(arg_keys[8], (D, H * HD), D ** -0.5, 0.125, ((0, 32),))
    w_out = noise(arg_keys[9], (D, H * HD), (D * 16 // SEQ) ** -0.5, 0.75, ((0, 32),))
    w_gate = noise(arg_keys[10], (D, FF), D ** -0.5, 0.125, ((0, 32),))
    w_up = noise(arg_keys[11], (D, FF), D ** -0.5, 0.125, ((0, 32),))
    w_down = noise(arg_keys[12], (D, FF), FF ** -0.5, 0.078125, ((0, 32),))
    cotangent = noise_with(arg_keys[13], (ROWS, SEQ, D), 1.0, 6.0, ((0, 4), (1, 8)), (1, 2, 8, 2.0))
    return dict(tokens=tokens, memory=memory, lengths=lengths, gain_attn=gain_attn, gain_memory=gain_memory, gain_ffn=gain_ffn, w_query=w_query, w_key=w_key, w_value=w_value, w_out=w_out, w_gate=w_gate, w_up=w_up, w_down=w_down, cotangent=cotangent)


epsilon = 1e-06
negative = -1e+30
highest = lax.Precision.HIGHEST

@jax.custom_vjp
def low(v):
    return lax.optimization_barrier(v.astype(jnp.bfloat16)).astype(jnp.float32)

@jax.custom_vjp
def low_back(v):
    return v

def low_keep(v):
    return (low(v), None)

def low_pass(kept, grad):
    return (grad,)

def back_keep(v):
    return (v, None)

def back_low(kept, grad):
    return (low(grad),)
low.defvjp(low_keep, low_pass)
low_back.defvjp(back_keep, back_low)

def matmul_high(left, right):
    return jnp.dot(left, right, precision=highest, preferred_element_type=jnp.float32)

def normalize(values):
    return values * lax.rsqrt(lax.optimization_barrier(jnp.mean(values * values, axis=-1, keepdims=True)) + epsilon)

def segment_ids(lengths_row, length):
    boundaries = jnp.cumsum(lengths_row).astype(jnp.int32)
    places = jnp.arange(length, dtype=jnp.int32)
    numbers = lax.optimization_barrier(jnp.sum((places[:, None] >= boundaries[None, :]).astype(jnp.int32), axis=1))
    return jnp.where(places < boundaries[-1], numbers, -1).astype(jnp.int32)

def attention_row(queries, key_rows, value_rows, segments):
    length = queries.shape[0]
    block_rows = min(512, length)
    places = jnp.arange(length, dtype=jnp.int32)
    score_scale = queries.shape[-1] ** (-0.5)

    def one_block(block_index):
        first_row = (block_index * block_rows).astype(jnp.int32)
        query_block = lax.dynamic_slice_in_dim(queries, first_row, block_rows, 0)
        block_places = lax.dynamic_slice_in_dim(places, first_row, block_rows, 0)
        block_segments = lax.dynamic_slice_in_dim(segments, first_row, block_rows, 0)
        scores = low_back(jnp.einsum('qhd,khd->hqk', query_block, key_rows, precision=highest) * score_scale)
        allowed = (block_segments[:, None] == segments[None, :]) & (places[None, :] <= block_places[:, None])
        scores = jnp.where(allowed[None], scores, negative)
        largest = lax.optimization_barrier(jnp.max(scores, axis=-1, keepdims=True))
        exponent = jnp.exp(scores - largest)
        weights = exponent / lax.optimization_barrier(jnp.sum(exponent, axis=-1, keepdims=True))
        return jnp.einsum('hqk,khd->qhd', low(weights), value_rows, precision=highest)
    mixed_heads = lax.map(jax.checkpoint(one_block), jnp.arange(length // block_rows, dtype=jnp.int32))
    return mixed_heads.reshape(length, -1)

def layer_row(tokens, memory, segments, gain_attn, gain_memory, gain_ffn, w_query, w_key, w_value, w_out, w_gate, w_up, w_down):
    length = tokens.shape[0]
    token_in = low(normalize(tokens) * gain_attn)
    memory_in = low(normalize(memory) * gain_memory)
    queries = low_back(low(matmul_high(token_in, w_query))).reshape(length, H, HD)
    key_rows = low_back(low(matmul_high(memory_in, w_key))).reshape(length, H, HD)
    value_rows = low_back(low(matmul_high(memory_in, w_value))).reshape(length, H, HD)
    mixed_heads = attention_row(queries, key_rows, value_rows, segments)
    attended = low_back(low(mixed_heads))
    residual = tokens + low_back(matmul_high(attended, w_out.T))
    ffn_in = low(normalize(residual) * gain_ffn)
    gate_values = low_back(matmul_high(ffn_in, w_gate))
    up_values = low_back(matmul_high(ffn_in, w_up))
    hidden = low(jax.nn.silu(gate_values) * up_values)
    return residual + low_back(matmul_high(hidden, w_down.T))

def forward(tokens, memory, gain_attn, gain_memory, gain_ffn, w_query, w_key, w_value, w_out, w_gate, w_up, w_down, segments):

    def one_row(row_inputs):
        token_row, memory_row, segment_row = row_inputs
        return layer_row(token_row, memory_row, segment_row, gain_attn, gain_memory, gain_ffn, w_query, w_key, w_value, w_out, w_gate, w_up, w_down)
    return lax.map(one_row, (tokens, memory, segments))

def reference(tokens, memory, lengths, gain_attn, gain_memory, gain_ffn, w_query, w_key, w_value, w_out, w_gate, w_up, w_down, cotangent):
    segments = jax.vmap(lambda lengths_row: segment_ids(lengths_row, SEQ))(lengths)
    floats = [array.astype(jnp.float32) for array in (tokens, memory, gain_attn, gain_memory, gain_ffn, w_query, w_key, w_value, w_out, w_gate, w_up, w_down)]
    output, pull_back = jax.vjp(lambda *values: forward(*values, segments), *floats)
    valid = (segments >= 0).astype(jnp.float32)[..., None]
    grads = pull_back(cotangent.astype(jnp.float32) * valid)
    return (output.astype(jnp.bfloat16), grads[0].astype(jnp.bfloat16), grads[1].astype(jnp.bfloat16), grads[2], grads[3], grads[4], grads[5], grads[6], grads[7], grads[8], grads[9], grads[10], grads[11])
```

```python
import functools

import jax
import jax.numpy as jnp
from jax import lax
from jax.experimental import pallas as pl
from jax.experimental.pallas import tpu as pltpu
from jax.sharding import PartitionSpec as P

H = 16
HD = 128
AXES = ("dp", "ulysses", "blk")
bf16 = jnp.bfloat16
f32 = jnp.float32
epsilon = 1e-06
negative = -1e30


def dot(left, right, over, kind=f32):
    return lax.dot_general(left, right, (over, ((), ())), preferred_element_type=kind)


def times(left, right, kind=f32):
    return dot(left, right, ((1,), (0,)), kind)


def times_transposed(left, right, kind=f32):
    return dot(left, right, ((1,), (1,)), kind)


def transposed_times(left, right, kind=f32):
    return dot(left, right, ((0,), (0,)), kind)


def normalize(values):
    inverse = lax.rsqrt(jnp.mean(values * values, axis=-1, keepdims=True) + epsilon)
    return (values * inverse, inverse)


def norm_back(grad_normed, normed, inverse, gain):
    scaled = grad_normed * gain
    return inverse * (scaled - normed * jnp.mean(scaled * normed, axis=-1, keepdims=True))


def add_low(left, right):
    return (left.astype(f32) + right.astype(f32)).astype(bf16)


def masked_scores(q, k, start, place, key_place, scale):
    scores = times_transposed(q, k) * scale
    allowed = (key_place >= start) & (key_place <= place)
    return jnp.where(allowed, scores, negative)


def attention_parts(q_ref, k_ref, ko_ref, info_ref, places_ref, scale):
    width = q_ref.shape[-1]
    q = q_ref[0, :, 0].reshape(-1, width)
    k = k_ref[0, :, 0].reshape(-1, width)
    ko = ko_ref[0, :, 0].reshape(-1, width)
    start = info_ref[0, 0, :, 0:1]
    place = info_ref[0, 0, :, 1:2]
    own = masked_scores(q, k, start, place, places_ref[0:1, :], scale)
    other = masked_scores(q, ko, start, place, places_ref[1:2, :], scale)
    largest = jnp.maximum(
        jnp.max(own, axis=-1, keepdims=True), jnp.max(other, axis=-1, keepdims=True)
    )
    own = jnp.exp(own - largest)
    other = jnp.exp(other - largest)
    total = jnp.sum(own, axis=-1, keepdims=True) + jnp.sum(other, axis=-1, keepdims=True)
    return q, k, ko, own / total, other / total


def attend_kernel(scale, q_ref, k_ref, v_ref, ko_ref, vo_ref, info_ref, places_ref, out_ref):
    width = q_ref.shape[-1]
    _, _, _, own, other = attention_parts(q_ref, k_ref, ko_ref, info_ref, places_ref, scale)
    v = v_ref[0, :, 0].reshape(-1, width)
    vo = vo_ref[0, :, 0].reshape(-1, width)
    mixed = times(own.astype(bf16), v) + times(other.astype(bf16), vo)
    out_ref[0, :, 0] = mixed.astype(bf16).reshape(out_ref.shape[1], out_ref.shape[3], width)


def attend_back_kernel(
    scale,
    q_ref,
    k_ref,
    v_ref,
    ko_ref,
    vo_ref,
    g_ref,
    info_ref,
    places_ref,
    gq_ref,
    gk_ref,
    gv_ref,
    gko_ref,
    gvo_ref,
):
    width = q_ref.shape[-1]
    q, k, ko, own, other = attention_parts(q_ref, k_ref, ko_ref, info_ref, places_ref, scale)
    v = v_ref[0, :, 0].reshape(-1, width)
    vo = vo_ref[0, :, 0].reshape(-1, width)
    g = g_ref[0, :, 0].reshape(-1, width)
    grad_own = times_transposed(g, v)
    grad_other = times_transposed(g, vo)
    centre = jnp.sum(own * grad_own, axis=-1, keepdims=True) + jnp.sum(
        other * grad_other, axis=-1, keepdims=True
    )
    score_own = (own * (grad_own - centre)).astype(bf16)
    score_other = (other * (grad_other - centre)).astype(bf16)

    def put(ref, value):
        ref[0, :, 0] = value.astype(ref.dtype).reshape(ref.shape[1], ref.shape[3], width)

    put(gq_ref, (times(score_own, k) + times(score_other, ko)) * scale)
    put(gk_ref, transposed_times(score_own, q) * scale)
    put(gko_ref, transposed_times(score_other, q) * scale)
    put(gv_ref, transposed_times(own.astype(bf16), g))
    put(gvo_ref, transposed_times(other.astype(bf16), g))


def attention_call(kernel, inputs, info, places, out_kinds):
    twins, pieces, rows, tok, width = inputs[0].shape
    heads = width // HD
    block = pl.BlockSpec((1, pieces, 1, tok, HD), lambda c, r, h: (c, 0, r, 0, h))
    span = pieces * tok
    flops = 2 * twins * rows * heads * span * span * HD * 2 * len(inputs)
    return pl.pallas_call(
        kernel,
        grid=(twins, rows, heads),
        in_specs=[block] * len(inputs)
        + [
            pl.BlockSpec((1, 1, span, 2), lambda c, r, h: (c, r, 0, 0)),
            pl.BlockSpec(places.shape, lambda c, r, h: (0, 0)),
        ],
        out_specs=[block] * len(out_kinds),
        out_shape=[jax.ShapeDtypeStruct(inputs[0].shape, kind) for kind in out_kinds],
        compiler_params=pltpu.CompilerParams(vmem_limit_bytes=48 * 1024 * 1024),
        cost_estimate=pl.CostEstimate(
            flops=flops,
            bytes_accessed=2 * inputs[0].size * (len(inputs) + len(out_kinds)),
            transcendentals=2 * twins * rows * heads * span * span,
        ),
    )(*inputs, info, places)


class Places:
    def __init__(self):
        self.dp, self.ul, self.blk = (lax.axis_size(axis) for axis in AXES)
        self.count = self.dp * self.ul * self.blk
        self.me = (
            lax.axis_index("dp") * self.ul + lax.axis_index("ulysses")
        ) * self.blk + lax.axis_index("blk")
        self.group = self.ul * self.blk
        self.half_bit = self.group // 2
        self.twin_bit = self.group
        self.far_bit = 2 * self.group
        self.inner = [1 << i for i in range(self.half_bit.bit_length() - 1)]

    def bit(self, mask):
        return (self.me // mask) % 2

    def swap(self, value, mask):
        return lax.ppermute(value, AXES, [(i, i ^ mask) for i in range(self.count)])

    def send(self, value, mask, chosen):
        return lax.ppermute(
            value, AXES, [(i, i ^ mask) for i in range(self.count) if chosen(i)]
        )

    def block(self):
        return self.bit(self.twin_bit) * self.half_bit + self.me % self.half_bit

    def members(self):
        for place in range(self.group):
            twin, low = divmod(place, self.half_bit)
            yield place, twin * self.twin_bit + low


def split_weights(at, weights):
    rows, width = weights[0].shape
    cols = width // at.group
    return jnp.stack(
        [w.reshape(rows, at.group, cols).transpose(1, 0, 2) for w in weights], axis=1
    )


def column_weights(at, weights):
    blocks = split_weights(at, weights)
    group, number, rows, cols = blocks.shape
    mine = at.block()
    near = jnp.zeros((number, group, rows, cols), bf16)
    for place, mask in at.members():
        piece = lax.dynamic_index_in_dim(blocks, mine ^ place, 0, keepdims=False)
        if mask:
            piece = at.swap(piece, mask)
        near = lax.dynamic_update_slice(near, piece[:, None], (0, mine ^ place, 0, 0))
    low = group // 2 * rows
    near = near.reshape(number, 2, low, cols)
    half = at.swap(near, at.half_bit)
    far = at.swap(near, at.far_bit)
    far_half = at.swap(half, at.far_bit)
    out = jnp.zeros((number, at.dp // 2, 2, 2, low, cols), bf16)
    x, z = at.bit(at.far_bit), at.bit(at.half_bit)
    for value, there, across in ((near, x, z), (half, x, 1 - z), (far, 1 - x, z), (far_half, 1 - x, 1 - z)):
        out = lax.dynamic_update_slice(
            out, value[:, None, :, None], (0, there, 0, across, 0, 0)
        )
    return out.reshape(number, -1, cols)


def gather(at, value):
    slots = {0: value}
    for mask in at.inner[2:]:
        for s in list(slots):
            slots[s ^ mask] = at.swap(slots[s], mask)
    cut = value.shape[0] // 2
    for s in list(slots):
        own = slots[s]
        by_y = at.swap(own, 1)
        by_z = at.swap(own, 2)
        first = at.swap(by_z[:cut], 1)
        second = at.swap(by_y[cut:], 2)
        slots[s ^ 1], slots[s ^ 2] = by_y, by_z
        slots[s ^ 3] = jnp.concatenate([first, second])
    whole = jnp.stack([slots[s] for s in range(at.half_bit)])
    return jnp.concatenate([whole, at.swap(whole, at.twin_bit)])


def scatter(at, terms):
    low = at.half_bit
    kept = add_low(terms[:low], at.swap(terms[low:], at.twin_bit))
    slots = {s: kept[s] for s in range(low)}
    for mask in reversed(at.inner[2:]):
        for s in [s for s in slots if s & mask]:
            slots[s ^ mask] = add_low(slots[s ^ mask], at.swap(slots.pop(s), mask))
    cut = terms.shape[1] // 2
    first = at.swap(slots[3][:cut], 1)
    second = at.swap(slots[3][cut:], 2)
    to_z = jnp.concatenate([add_low(slots[2][:cut], first), slots[2][cut:]])
    to_y = jnp.concatenate([slots[1][:cut], add_low(slots[1][cut:], second)])
    return (
        slots[0].astype(f32)
        + at.swap(to_y, 1).astype(f32)
        + at.swap(to_z, 2).astype(f32)
    )


def reduce_gradient(at, terms):
    number, rows, cols = terms.shape
    x, z, twin = at.bit(at.far_bit), at.bit(at.half_bit), at.bit(at.twin_bit)
    terms = terms.reshape(number, 2, rows // 2, cols)
    there = lax.dynamic_index_in_dim(terms, 1 - x, 1, keepdims=False)
    here = lax.dynamic_index_in_dim(terms, x, 1, keepdims=False)
    kept = add_low(here, at.swap(there, at.far_bit))

    def away(i):
        return (i // at.half_bit) % 2 != (i // at.twin_bit) % 2

    both = kept.astype(f32) + at.send(kept, at.half_bit, away).astype(f32)
    both = both.reshape(number, 2, rows // 4, cols)
    mine = lax.dynamic_index_in_dim(both, twin, 1, keepdims=False)
    twins = lax.dynamic_index_in_dim(both, 1 - twin, 1, keepdims=False)
    given = at.send(twins.astype(bf16), at.twin_bit, lambda i: not away(i))
    return jnp.where(z == twin, mine, given.astype(f32))


def reduce_gains(at, terms):
    mask = at.count // 2
    while mask:
        terms = terms.reshape(terms.shape[0], 2, -1)
        upper = at.bit(mask)
        there = lax.dynamic_index_in_dim(terms, 1 - upper, 1, keepdims=False)
        here = lax.dynamic_index_in_dim(terms, upper, 1, keepdims=False)
        terms = here + at.swap(there, mask)
        mask //= 2
    return terms


def on_device(
    tokens,
    memory,
    lengths,
    gain_attn,
    gain_memory,
    gain_ffn,
    w_query,
    w_key,
    w_value,
    w_out,
    w_gate,
    w_up,
    w_down,
    cotangent,
):
    at = Places()
    rows_here, tok_row, model_width = tokens.shape
    count = rows_here * tok_row
    group = at.group
    half = group // 2
    head_width = w_query.shape[1]
    own_width = head_width // group
    width = max(own_width, HD)
    row_length = tok_row * at.ul * at.blk
    scale = HD ** (-0.5)

    bounds = jnp.cumsum(lengths, axis=1)
    all_bounds = jnp.stack([bounds, at.swap(bounds, at.twin_bit)])
    position = at.me % group
    own_places = ((position ^ jnp.arange(half, dtype=jnp.int32))[:, None] * tok_row
                  + jnp.arange(tok_row, dtype=jnp.int32)[None]).reshape(-1)
    other_places = ((position ^ half ^ jnp.arange(half, dtype=jnp.int32))[:, None] * tok_row
                    + jnp.arange(tok_row, dtype=jnp.int32)[None]).reshape(-1)
    passed = all_bounds[:, :, None, :] <= own_places[None, None, :, None]
    starts = jnp.max(jnp.where(passed, all_bounds[:, :, None, :], 0), axis=-1)
    info = jnp.stack([starts, jnp.broadcast_to(own_places, starts.shape)], axis=-1)
    key_places = jnp.stack([own_places, other_places])
    here = position * tok_row + jnp.arange(tok_row, dtype=jnp.int32)
    valid = (here[None] < bounds[:, -1:]).astype(f32).reshape(count, 1)

    residual_in = tokens.reshape(count, model_width).astype(f32)
    token_normed, token_inverse = normalize(residual_in)
    token_in = (token_normed * gain_attn).astype(bf16)
    memory_normed, memory_inverse = normalize(memory.reshape(count, model_width).astype(f32))
    memory_in = (memory_normed * gain_memory).astype(bf16)
    grad_final = cotangent.reshape(count, model_width).astype(f32) * valid

    def flat(value):
        return value.reshape(group * count, -1)

    def slots(value):
        return value.reshape(group, count, -1)

    def widen(value):
        if own_width >= HD:
            return value
        mask = 1
        while value.shape[1] < HD:
            given = at.swap(value, mask)
            given = given.reshape(-1, 2, mask * count, given.shape[1])[:, ::-1].reshape(given.shape)
            first = at.bit(mask) == 0
            value = jnp.concatenate(
                [jnp.where(first, value, given), jnp.where(first, given, value)], axis=1
            )
            mask *= 2
        return value

    def narrow(value):
        if own_width >= HD:
            return value
        return lax.dynamic_slice_in_dim(
            value, at.me % (HD // own_width) * own_width, own_width, axis=1
        )

    def heads(value):
        return value.reshape(2, half, rows_here, tok_row, width)

    attn_w = column_weights(at, [w_query, w_key, w_value])
    memory_all = flat(gather(at, memory_in))
    token_all = flat(gather(at, token_in))
    out_w = column_weights(at, [w_out])[0]

    def first_half(i):
        return (i // at.half_bit) % 2 == 0

    def second_half(i):
        return not first_half(i)

    keys = heads(widen(times(memory_all, attn_w[1], bf16)))
    values = heads(widen(times(memory_all, attn_w[2], bf16)))
    other_keys = at.send(keys, at.half_bit, first_half)
    other_values = at.send(values, at.half_bit, first_half)
    queries = heads(widen(times(token_all, attn_w[0], bf16)))
    (mixed,) = attention_call(
        functools.partial(attend_kernel, scale),
        [queries, keys, values, other_keys, other_values],
        info,
        key_places,
        [bf16],
    )
    mixed = narrow(mixed.reshape(group * count, width))

    gate_w, up_w = column_weights(at, [w_gate, w_up])
    (down_w,) = column_weights(at, [w_down])
    final_all = flat(gather(at, grad_final.astype(bf16)))

    residual = residual_in + scatter(at, slots(times_transposed(mixed, out_w, bf16)))
    ffn_normed, ffn_inverse = normalize(residual)
    ffn_in = (ffn_normed * gain_ffn).astype(bf16)
    ffn_all = flat(gather(at, ffn_in))
    gate = times(ffn_all, gate_w)
    up = times(ffn_all, up_w)
    grad_hidden = times(final_all, down_w)
    gate_sigmoid = jax.nn.sigmoid(gate)
    silu = gate * gate_sigmoid
    hidden = (silu * up).astype(bf16)
    grad_gate_in = (
        grad_hidden * up * gate_sigmoid * (1.0 + gate * (1.0 - gate_sigmoid))
    ).astype(bf16)
    grad_up_in = (grad_hidden * silu).astype(bf16)
    grad_ffn_in = scatter(
        at,
        slots(
            (times_transposed(grad_gate_in, gate_w) + times_transposed(grad_up_in, up_w)).astype(
                bf16
            )
        ),
    )
    grad_residual = grad_final + norm_back(grad_ffn_in, ffn_normed, ffn_inverse, gain_ffn)
    grad_branch = grad_residual.astype(bf16)
    branch_all = flat(gather(at, grad_branch))
    grad_mixed = heads(widen(times(branch_all, out_w, bf16)))
    grad_queries, grad_keys, grad_values, grad_other_keys, grad_other_values = attention_call(
        functools.partial(attend_back_kernel, scale),
        [queries, keys, values, other_keys, other_values, grad_mixed],
        info,
        key_places,
        [bf16, f32, f32, bf16, bf16],
    )
    given_keys = at.send(grad_other_keys, at.half_bit, second_half)
    given_values = at.send(grad_other_values, at.half_bit, second_half)
    grad_queries = narrow(grad_queries.reshape(group * count, width))

    output = residual + scatter(at, slots(times_transposed(hidden, down_w, bf16)))

    down_term = transposed_times(final_all, hidden, bf16)
    gate_term = transposed_times(ffn_all, grad_gate_in, bf16)
    up_term = transposed_times(ffn_all, grad_up_in, bf16)
    ffn_grads = reduce_gradient(at, jnp.stack([gate_term, up_term, down_term]))

    grad_token_in = scatter(at, slots(times_transposed(grad_queries, attn_w[0], bf16)))
    grad_keys = narrow(
        (grad_keys + given_keys.astype(f32)).astype(bf16).reshape(group * count, width)
    )
    grad_values = narrow(
        (grad_values + given_values.astype(f32)).astype(bf16).reshape(group * count, width)
    )
    grad_memory_in = scatter(
        at,
        slots(
            (
                times_transposed(grad_keys, attn_w[1]) + times_transposed(grad_values, attn_w[2])
            ).astype(bf16)
        ),
    )
    query_term = transposed_times(token_all, grad_queries, bf16)
    out_term = transposed_times(branch_all, mixed, bf16)
    key_term = transposed_times(memory_all, grad_keys, bf16)
    value_term = transposed_times(memory_all, grad_values, bf16)
    attn_grads = reduce_gradient(at, jnp.stack([query_term, key_term, value_term, out_term]))

    def against(term, weight):
        return jnp.sum(term.astype(f32) * weight.astype(f32), axis=1)

    gain_terms = jnp.stack(
        [
            against(query_term, attn_w[0]) / gain_attn,
            (against(key_term, attn_w[1]) + against(value_term, attn_w[2])) / gain_memory,
            (against(gate_term, gate_w) + against(up_term, up_w)) / gain_ffn,
        ]
    )
    gain_grads = reduce_gains(at, gain_terms)

    grad_tokens = grad_residual + norm_back(grad_token_in, token_normed, token_inverse, gain_attn)
    grad_memory = norm_back(grad_memory_in, memory_normed, memory_inverse, gain_memory)
    shape = (rows_here, tok_row, model_width)
    return (
        output.astype(bf16).reshape(shape),
        grad_tokens.astype(bf16).reshape(shape),
        grad_memory.astype(bf16).reshape(shape),
        gain_grads[0],
        gain_grads[1],
        gain_grads[2],
        attn_grads[0],
        attn_grads[1],
        attn_grads[2],
        attn_grads[3],
        ffn_grads[0],
        ffn_grads[1],
        ffn_grads[2],
    )


def solution(mesh):
    rows = P("dp", ("ulysses", "blk"), None)
    weight = P(AXES, None)
    grad = P("dp", ("ulysses", "blk"))
    return jax.shard_map(
        on_device,
        mesh=mesh,
        in_specs=(rows, rows, P("dp", None), P(), P(), P()) + (weight,) * 7 + (rows,),
        out_specs=(rows,) * 3 + (P(AXES),) * 3 + (grad,) * 7,
        check_vma=False,
    )
```

```python
import functools

import jax
import jax.numpy as jnp
from jax import lax
from jax.experimental import pallas as pl
from jax.experimental.pallas import tpu as pltpu
from jax.sharding import PartitionSpec as P

H = 16
HD = 128
AXES = ("dp", "ulysses", "blk")
bf16 = jnp.bfloat16
f32 = jnp.float32
epsilon = 1e-06
negative = -1e30


def dot(left, right, over, kind=f32):
    return lax.dot_general(left, right, (over, ((), ())), preferred_element_type=kind)


def times(left, right, kind=f32):
    return dot(left, right, ((1,), (0,)), kind)


def times_transposed(left, right, kind=f32):
    return dot(left, right, ((1,), (1,)), kind)


def transposed_times(left, right, kind=f32):
    return dot(left, right, ((0,), (0,)), kind)


def normalize(values):
    inverse = lax.rsqrt(jnp.mean(values * values, axis=-1, keepdims=True) + epsilon)
    return (values * inverse, inverse)


def norm_back(grad_normed, normed, inverse, gain):
    scaled = grad_normed * gain
    return inverse * (scaled - normed * jnp.mean(scaled * normed, axis=-1, keepdims=True))


def add_low(left, right):
    return (left.astype(f32) + right.astype(f32)).astype(bf16)


def masked_scores(q, k, start, place, key_place, scale):
    scores = times_transposed(q, k) * scale
    allowed = (key_place >= start) & (key_place <= place)
    return jnp.where(allowed, scores, negative)


def attention_parts(q_ref, k_ref, ko_ref, info_ref, places_ref, scale):
    width = q_ref.shape[-1]
    q = q_ref[0, :, 0].reshape(-1, width)
    k = k_ref[0, :, 0].reshape(-1, width)
    ko = ko_ref[0, :, 0].reshape(-1, width)
    start = info_ref[0, 0, :, 0:1]
    place = info_ref[0, 0, :, 1:2]
    own = masked_scores(q, k, start, place, places_ref[0:1, :], scale)
    other = masked_scores(q, ko, start, place, places_ref[1:2, :], scale)
    largest = jnp.maximum(
        jnp.max(own, axis=-1, keepdims=True), jnp.max(other, axis=-1, keepdims=True)
    )
    own = jnp.exp(own - largest)
    other = jnp.exp(other - largest)
    total = jnp.sum(own, axis=-1, keepdims=True) + jnp.sum(other, axis=-1, keepdims=True)
    return q, k, ko, own / total, other / total


def attend_kernel(scale, q_ref, k_ref, v_ref, ko_ref, vo_ref, info_ref, places_ref, out_ref):
    width = q_ref.shape[-1]
    _, _, _, own, other = attention_parts(q_ref, k_ref, ko_ref, info_ref, places_ref, scale)
    v = v_ref[0, :, 0].reshape(-1, width)
    vo = vo_ref[0, :, 0].reshape(-1, width)
    mixed = times(own.astype(bf16), v) + times(other.astype(bf16), vo)
    out_ref[0, :, 0] = mixed.astype(bf16).reshape(out_ref.shape[1], out_ref.shape[3], width)


def attend_back_kernel(
    scale,
    q_ref,
    k_ref,
    v_ref,
    ko_ref,
    vo_ref,
    g_ref,
    info_ref,
    places_ref,
    gq_ref,
    gk_ref,
    gv_ref,
    gko_ref,
    gvo_ref,
):
    width = q_ref.shape[-1]
    q, k, ko, own, other = attention_parts(q_ref, k_ref, ko_ref, info_ref, places_ref, scale)
    v = v_ref[0, :, 0].reshape(-1, width)
    vo = vo_ref[0, :, 0].reshape(-1, width)
    g = g_ref[0, :, 0].reshape(-1, width)
    grad_own = times_transposed(g, v)
    grad_other = times_transposed(g, vo)
    centre = jnp.sum(own * grad_own, axis=-1, keepdims=True) + jnp.sum(
        other * grad_other, axis=-1, keepdims=True
    )
    score_own = (own * (grad_own - centre)).astype(bf16)
    score_other = (other * (grad_other - centre)).astype(bf16)

    def put(ref, value):
        ref[0, :, 0] = value.astype(ref.dtype).reshape(ref.shape[1], ref.shape[3], width)

    put(gq_ref, (times(score_own, k) + times(score_other, ko)) * scale)
    put(gk_ref, transposed_times(score_own, q) * scale)
    put(gko_ref, transposed_times(score_other, q) * scale)
    put(gv_ref, transposed_times(own.astype(bf16), g))
    put(gvo_ref, transposed_times(other.astype(bf16), g))


def attention_call(kernel, inputs, info, places, out_kinds):
    twins, pieces, rows, tok, width = inputs[0].shape
    heads = width // HD
    block = pl.BlockSpec((1, pieces, 1, tok, HD), lambda c, r, h: (c, 0, r, 0, h))
    span = pieces * tok
    flops = 2 * twins * rows * heads * span * span * HD * 2 * len(inputs)
    return pl.pallas_call(
        kernel,
        grid=(twins, rows, heads),
        in_specs=[block] * len(inputs)
        + [
            pl.BlockSpec((1, 1, span, 2), lambda c, r, h: (c, r, 0, 0)),
            pl.BlockSpec(places.shape, lambda c, r, h: (0, 0)),
        ],
        out_specs=[block] * len(out_kinds),
        out_shape=[jax.ShapeDtypeStruct(inputs[0].shape, kind) for kind in out_kinds],
        compiler_params=pltpu.CompilerParams(vmem_limit_bytes=48 * 1024 * 1024),
        cost_estimate=pl.CostEstimate(
            flops=flops,
            bytes_accessed=2 * inputs[0].size * (len(inputs) + len(out_kinds)),
            transcendentals=2 * twins * rows * heads * span * span,
        ),
    )(*inputs, info, places)


def exchange_blocks(blocks, flags):
    for i, flag in enumerate(flags):
        mask = 1 << i
        blocks = [jnp.where(flag, blocks[j ^ mask], blocks[j]) for j in range(len(blocks))]
    return blocks


def flags_of(number, bits):
    return [((number >> i) & 1) == 1 for i in range(bits)]


def split_kernel(weights, group, me_ref, *refs):
    flags = flags_of(me_ref[0], group.bit_length() - 1)
    for i in range(weights):
        cols = refs[i].shape[1] // group
        blocks = [refs[i][:, j * cols : (j + 1) * cols] for j in range(group)]
        for ref, block in zip(refs[weights:], exchange_blocks(blocks, flags)):
            ref[i] = block


def place_kernel(group, me_ref, *refs):
    flags = flags_of(me_ref[0], group.bit_length() - 1)
    out = refs[group]
    rows = refs[0].shape[1]
    for i in range(out.shape[0]):
        blocks = exchange_blocks([ref[i] for ref in refs[:group]], flags)
        for j, block in enumerate(blocks):
            out[i, j * rows : (j + 1) * rows] = block


def permuted(value, flags):
    low = value.shape[1] // 8
    blocks = [value[:, i * low : (i + 1) * low] for i in (0, 2, 1, 3, 4, 6, 5, 7)]
    for mask, flag in ((2, flags[0]), (4, flags[1])):
        blocks = [jnp.where(flag, blocks[j ^ mask], blocks[j]) for j in range(8)]
    return blocks


def restored(value, flags):
    low = value.shape[1] // 8
    blocks = [value[:, i * low : (i + 1) * low] for i in range(8)]
    for mask, flag in ((2, flags[0]), (4, flags[1])):
        blocks = [jnp.where(flag, blocks[j ^ mask], blocks[j]) for j in range(8)]
    return [blocks[i] for i in (0, 2, 1, 3, 4, 6, 5, 7)]


def move_kernel(how, me_ref, *refs):
    flags = [me_ref[0] == 1, me_ref[1] == 1]
    number = len(refs) // 2
    for source, target in zip(refs[:number], refs[number:]):
        low = source.shape[1] // 8
        for i, block in enumerate(how(source[...], flags)):
            target[:, i * low : (i + 1) * low] = block


def local_call(kernel, scalars, inputs, outputs):
    vmem = pl.BlockSpec(memory_space=pltpu.VMEM)
    size = sum(a.size * a.dtype.itemsize for a in [*inputs, *outputs])
    return pl.pallas_call(
        kernel,
        in_specs=[pl.BlockSpec(memory_space=pltpu.SMEM)] + [vmem] * len(inputs),
        out_specs=[vmem] * len(outputs),
        out_shape=outputs,
        compiler_params=pltpu.CompilerParams(vmem_limit_bytes=48 * 1024 * 1024),
        cost_estimate=pl.CostEstimate(flops=0, bytes_accessed=size, transcendentals=0),
    )(scalars, *inputs)


class Places:
    def __init__(self):
        self.dp, self.ul, self.blk = (lax.axis_size(axis) for axis in AXES)
        self.count = self.dp * self.ul * self.blk
        self.me = (
            lax.axis_index("dp") * self.ul + lax.axis_index("ulysses")
        ) * self.blk + lax.axis_index("blk")
        self.group = self.ul * self.blk
        self.half_bit = self.group // 2
        self.twin_bit = self.group
        self.far_bit = 2 * self.group
        self.inner = [1 << i for i in range(self.half_bit.bit_length() - 1)]

    def bit(self, mask):
        return (self.me // mask) % 2

    def swap(self, value, mask):
        return lax.ppermute(value, AXES, [(i, i ^ mask) for i in range(self.count)])

    def send(self, value, mask, chosen):
        return lax.ppermute(
            value, AXES, [(i, i ^ mask) for i in range(self.count) if chosen(i)]
        )

    def block(self):
        return self.bit(self.twin_bit) * self.half_bit + self.me % self.half_bit

    def members(self):
        for place in range(self.group):
            twin, low = divmod(place, self.half_bit)
            yield place, twin * self.twin_bit + low


def column_weights(at, weights):
    rows, width = weights[0].shape
    number, cols = len(weights), width // at.group
    shape = jax.ShapeDtypeStruct((number, rows, cols), bf16)
    mine = at.block().astype(jnp.int32).reshape(1)
    pieces = local_call(
        functools.partial(split_kernel, number, at.group), mine, weights, [shape] * at.group
    )
    pieces = [
        at.swap(piece, mask) if mask else piece for piece, (_, mask) in zip(pieces, at.members())
    ]
    near = local_call(
        functools.partial(place_kernel, at.group),
        mine,
        pieces,
        [jax.ShapeDtypeStruct((number, at.group * rows, cols), bf16)],
    )[0]
    half = at.swap(near, at.half_bit)
    far = at.swap(near, at.far_bit)
    far_half = at.swap(half, at.far_bit)
    return [
        jnp.concatenate([part[i] for part in (near, half, far, far_half)], axis=0)
        for i in range(number)
    ]


def gather(at, value):
    slots = {0: [value]}
    for mask in at.inner[2:]:
        for s in list(slots):
            slots[s ^ mask] = [at.swap(slots[s][0], mask)]
    cut = value.shape[0] // 2
    for s in list(slots):
        (own,) = slots[s]
        by_y = at.swap(own, 1)
        by_z = at.swap(own, 2)
        first = at.swap(by_z[:cut], 1)
        second = at.swap(by_y[cut:], 2)
        slots[s ^ 1], slots[s ^ 2] = [by_y], [by_z]
        slots[s ^ 3] = [first, second]
    whole = jnp.concatenate([part for s in range(at.half_bit) for part in slots[s]], axis=0)
    return jnp.concatenate([whole, at.swap(whole, at.twin_bit)], axis=0)


def scatter(at, terms):
    low = at.half_bit
    tok = terms.shape[0] // at.group
    kept = add_low(terms[: low * tok], at.swap(terms[low * tok :], at.twin_bit))
    slots = {s: kept[s * tok : (s + 1) * tok] for s in range(low)}
    for mask in reversed(at.inner[2:]):
        for s in [s for s in slots if s & mask]:
            slots[s ^ mask] = add_low(slots[s ^ mask], at.swap(slots.pop(s), mask))
    cut = tok // 2
    first = at.swap(slots[3][:cut], 1)
    second = at.swap(slots[3][cut:], 2)
    to_z = jnp.concatenate([add_low(slots[2][:cut], first), slots[2][cut:]])
    to_y = jnp.concatenate([slots[1][:cut], add_low(slots[1][cut:], second)])
    return (
        slots[0].astype(f32)
        + at.swap(to_y, 1).astype(f32)
        + at.swap(to_z, 2).astype(f32)
    )


def reduce_gradient(at, terms):
    rows, cols = terms.shape
    z, twin = at.bit(at.half_bit), at.bit(at.twin_bit)
    kept = add_low(terms[: rows // 2], at.swap(terms[rows // 2 :], at.far_bit))

    def away(i):
        return (i // at.half_bit) % 2 != (i // at.twin_bit) % 2

    given = at.send(kept, at.half_bit, away).reshape(2, 2, rows // 8, cols)
    both = kept.reshape(2, 2, rows // 8, cols).astype(f32) + given[::-1].astype(f32)
    second = twin == 1
    mine = jnp.where(second, both[:, 1], both[:, 0])
    twins = jnp.where(second, both[:, 0], both[:, 1]).astype(bf16)
    given = at.send(twins, at.twin_bit, lambda i: not away(i))
    out = jnp.where(z == twin, mine, given.astype(f32))
    out = jnp.where(z == 1, out[::-1], out)
    return out.reshape(rows // 4, cols)


def reduce_gains(at, terms):
    for mask in (at.far_bit, at.half_bit):
        terms = terms.reshape(terms.shape[0], 2, -1)
        terms = terms[:, 0] + at.swap(terms[:, 1], mask)
    for mask in (at.twin_bit, *reversed(at.inner)):
        terms = terms.reshape(terms.shape[0], 2, -1)
        upper = at.bit(mask) == 1
        there = jnp.where(upper, terms[:, 0], terms[:, 1])
        here = jnp.where(upper, terms[:, 1], terms[:, 0])
        terms = here + at.swap(there, mask)
    return terms


def on_device(
    tokens,
    memory,
    lengths,
    gain_attn,
    gain_memory,
    gain_ffn,
    w_query,
    w_key,
    w_value,
    w_out,
    w_gate,
    w_up,
    w_down,
    cotangent,
):
    at = Places()
    rows_here, tok_row, model_width = tokens.shape
    count = rows_here * tok_row
    group = at.group
    half = group // 2
    head_width = w_query.shape[1]
    own_width = head_width // group
    width = max(own_width, HD)
    row_length = tok_row * at.ul * at.blk
    scale = HD ** (-0.5)

    bounds = jnp.cumsum(lengths, axis=1)
    all_bounds = jnp.stack([bounds, at.swap(bounds, at.twin_bit)])
    position = at.me % group
    own_places = ((position ^ jnp.arange(half, dtype=jnp.int32))[:, None] * tok_row
                  + jnp.arange(tok_row, dtype=jnp.int32)[None]).reshape(-1)
    other_places = ((position ^ half ^ jnp.arange(half, dtype=jnp.int32))[:, None] * tok_row
                    + jnp.arange(tok_row, dtype=jnp.int32)[None]).reshape(-1)
    passed = all_bounds[:, :, None, :] <= own_places[None, None, :, None]
    starts = jnp.max(jnp.where(passed, all_bounds[:, :, None, :], 0), axis=-1)
    info = jnp.stack([starts, jnp.broadcast_to(own_places, starts.shape)], axis=-1)
    key_places = jnp.stack([own_places, other_places])
    here = position * tok_row + jnp.arange(tok_row, dtype=jnp.int32)
    valid = (here[None] < bounds[:, -1:]).astype(f32).reshape(count, 1)

    attn_w = column_weights(at, [w_query, w_key, w_value])
    sides = jnp.stack([at.bit(at.half_bit), at.bit(at.far_bit)]).astype(jnp.int32)
    entry = [a.reshape(count, model_width) for a in (memory, tokens, cotangent)] + [
        gain.reshape(1, model_width) for gain in (gain_attn, gain_memory, gain_ffn)
    ]
    memory, tokens, cotangent, gain_attn, gain_memory, gain_ffn = local_call(
        functools.partial(move_kernel, permuted),
        sides,
        entry,
        [jax.ShapeDtypeStruct(a.shape, a.dtype) for a in entry],
    )
    residual_in = tokens.astype(f32)
    token_normed, token_inverse = normalize(residual_in)
    token_in = (token_normed * gain_attn).astype(bf16)
    memory_normed, memory_inverse = normalize(memory.astype(f32))
    memory_in = (memory_normed * gain_memory).astype(bf16)
    grad_final = cotangent.astype(f32) * valid

    def widen(value):
        if own_width >= HD:
            return value
        mask = 1
        while value.shape[1] < HD:
            given = at.swap(value, mask)
            given = given.reshape(-1, 2, mask * count, given.shape[1])[:, ::-1].reshape(given.shape)
            first = at.bit(mask) == 0
            value = jnp.concatenate(
                [jnp.where(first, value, given), jnp.where(first, given, value)], axis=1
            )
            mask *= 2
        return value

    def narrow(value):
        if own_width >= HD:
            return value
        return lax.dynamic_slice_in_dim(
            value, at.me % (HD // own_width) * own_width, own_width, axis=1
        )

    def heads(value):
        return value.reshape(2, half, rows_here, tok_row, width)

    memory_all = gather(at, memory_in)
    token_all = gather(at, token_in)
    (out_w,) = column_weights(at, [w_out])

    def first_half(i):
        return (i // at.half_bit) % 2 == 0

    def second_half(i):
        return not first_half(i)

    keys = heads(widen(times(memory_all, attn_w[1], bf16)))
    values = heads(widen(times(memory_all, attn_w[2], bf16)))
    other_keys = at.send(keys, at.half_bit, first_half)
    other_values = at.send(values, at.half_bit, first_half)
    queries = heads(widen(times(token_all, attn_w[0], bf16)))
    (mixed,) = attention_call(
        functools.partial(attend_kernel, scale),
        [queries, keys, values, other_keys, other_values],
        info,
        key_places,
        [bf16],
    )
    mixed = narrow(mixed.reshape(group * count, width))

    gate_w, up_w = column_weights(at, [w_gate, w_up])
    (down_w,) = column_weights(at, [w_down])
    final_all = gather(at, grad_final.astype(bf16))

    residual = residual_in + scatter(at, times_transposed(mixed, out_w, bf16))
    ffn_normed, ffn_inverse = normalize(residual)
    ffn_in = (ffn_normed * gain_ffn).astype(bf16)
    ffn_all = gather(at, ffn_in)
    gate = times(ffn_all, gate_w)
    up = times(ffn_all, up_w)
    grad_hidden = times(final_all, down_w)
    gate_sigmoid = jax.nn.sigmoid(gate)
    silu = gate * gate_sigmoid
    hidden = (silu * up).astype(bf16)
    grad_gate_in = (
        grad_hidden * up * gate_sigmoid * (1.0 + gate * (1.0 - gate_sigmoid))
    ).astype(bf16)
    grad_up_in = (grad_hidden * silu).astype(bf16)
    grad_ffn_in = scatter(
        at,
        (times_transposed(grad_gate_in, gate_w) + times_transposed(grad_up_in, up_w)).astype(bf16),
    )
    grad_residual = grad_final + norm_back(grad_ffn_in, ffn_normed, ffn_inverse, gain_ffn)
    grad_branch = grad_residual.astype(bf16)
    branch_all = gather(at, grad_branch)
    grad_mixed = heads(widen(times(branch_all, out_w, bf16)))
    grad_queries, grad_keys, grad_values, grad_other_keys, grad_other_values = attention_call(
        functools.partial(attend_back_kernel, scale),
        [queries, keys, values, other_keys, other_values, grad_mixed],
        info,
        key_places,
        [bf16, f32, f32, bf16, bf16],
    )
    given_keys = at.send(grad_other_keys, at.half_bit, second_half)
    given_values = at.send(grad_other_values, at.half_bit, second_half)
    grad_queries = narrow(grad_queries.reshape(group * count, width))

    output = residual + scatter(at, times_transposed(hidden, down_w, bf16))

    down_term = transposed_times(final_all, hidden, bf16)
    gate_term = transposed_times(ffn_all, grad_gate_in, bf16)
    up_term = transposed_times(ffn_all, grad_up_in, bf16)
    ffn_grads = [reduce_gradient(at, term) for term in (gate_term, up_term, down_term)]

    grad_token_in = scatter(at, times_transposed(grad_queries, attn_w[0], bf16))
    grad_keys = narrow(
        (grad_keys + given_keys.astype(f32)).astype(bf16).reshape(group * count, width)
    )
    grad_values = narrow(
        (grad_values + given_values.astype(f32)).astype(bf16).reshape(group * count, width)
    )
    grad_memory_in = scatter(
        at,
        (
            times_transposed(grad_keys, attn_w[1]) + times_transposed(grad_values, attn_w[2])
        ).astype(bf16),
    )
    query_term = transposed_times(token_all, grad_queries, bf16)
    out_term = transposed_times(branch_all, mixed, bf16)
    key_term = transposed_times(memory_all, grad_keys, bf16)
    value_term = transposed_times(memory_all, grad_values, bf16)
    attn_grads = [
        reduce_gradient(at, term) for term in (query_term, key_term, value_term, out_term)
    ]

    def against(term, weight):
        return jnp.sum(term.astype(f32) * weight.astype(f32), axis=1)

    gain_terms = jnp.stack(
        [
            against(query_term, attn_w[0]) / gain_attn[0],
            (against(key_term, attn_w[1]) + against(value_term, attn_w[2])) / gain_memory[0],
            (against(gate_term, gate_w) + against(up_term, up_w)) / gain_ffn[0],
        ]
    )
    gain_grads = reduce_gains(at, gain_terms)

    grad_tokens = grad_residual + norm_back(grad_token_in, token_normed, token_inverse, gain_attn)
    grad_memory = norm_back(grad_memory_in, memory_normed, memory_inverse, gain_memory)
    leaving = [a.astype(bf16) for a in (output, grad_tokens, grad_memory)]
    leaving = local_call(
        functools.partial(move_kernel, restored),
        sides,
        leaving,
        [jax.ShapeDtypeStruct(a.shape, a.dtype) for a in leaving],
    )
    output, grad_tokens, grad_memory = (
        a.reshape(rows_here, tok_row, model_width) for a in leaving
    )
    return (
        output,
        grad_tokens,
        grad_memory,
        gain_grads[0],
        gain_grads[1],
        gain_grads[2],
        attn_grads[0],
        attn_grads[1],
        attn_grads[2],
        attn_grads[3],
        ffn_grads[0],
        ffn_grads[1],
        ffn_grads[2],
    )


def solution(mesh):
    rows = P("dp", ("ulysses", "blk"), None)
    weight = P(AXES, None)
    grad = P("dp", ("ulysses", "blk"))
    return jax.shard_map(
        on_device,
        mesh=mesh,
        in_specs=(rows, rows, P("dp", None), P(), P(), P()) + (weight,) * 7 + (rows,),
        out_specs=(rows,) * 3 + (P(AXES),) * 3 + (grad,) * 7,
        check_vma=False,
    )
```

```python
import functools

import jax
import jax.numpy as jnp
from jax import lax
from jax.experimental import pallas as pl
from jax.experimental.pallas import tpu as pltpu
from jax.sharding import PartitionSpec as P

H = 16
HD = 128
AXES = ("dh", "dl", "uh", "ul", "blk")
GROUP = ("dl", "ul", "blk")
INNER = ("ul", "blk")
bf16 = jnp.bfloat16
f32 = jnp.float32
epsilon = 1e-06
negative = -1e30


def dot(left, right, over, kind=f32):
    return lax.dot_general(left, right, (over, ((), ())), preferred_element_type=kind)


def times(left, right, kind=f32):
    return dot(left, right, ((1,), (0,)), kind)


def times_transposed(left, right, kind=f32):
    return dot(left, right, ((1,), (1,)), kind)


def transposed_times(left, right, kind=f32):
    return dot(left, right, ((0,), (0,)), kind)


def normalize(values):
    inverse = lax.rsqrt(jnp.mean(values * values, axis=-1, keepdims=True) + epsilon)
    return (values * inverse, inverse)


def norm_back(grad_normed, normed, inverse, gain):
    scaled = grad_normed * gain
    return inverse * (scaled - normed * jnp.mean(scaled * normed, axis=-1, keepdims=True))


def add_low(left, right):
    return (left.astype(f32) + right.astype(f32)).astype(bf16)


def masked_scores(q, k, start, place, key_place, scale):
    scores = times_transposed(q, k) * scale
    allowed = (key_place >= start) & (key_place <= place)
    return jnp.where(allowed, scores, negative)


def attention_parts(q_ref, kv_ref, okv_ref, info_ref, places_ref, scale):
    q = q_ref[0, :, 0].reshape(-1, HD)
    kv = kv_ref[0, :, 0].reshape(-1, 2 * HD)
    okv = okv_ref[0, :, 0].reshape(-1, 2 * HD)
    start = info_ref[0, 0, :, 0:1]
    place = info_ref[0, 0, :, 1:2]
    own = masked_scores(q, kv[:, :HD], start, place, places_ref[0:1, :], scale)
    other = masked_scores(q, okv[:, :HD], start, place, places_ref[1:2, :], scale)
    largest = jnp.maximum(
        jnp.max(own, axis=-1, keepdims=True), jnp.max(other, axis=-1, keepdims=True)
    )
    own = jnp.exp(own - largest)
    other = jnp.exp(other - largest)
    total = jnp.sum(own, axis=-1, keepdims=True) + jnp.sum(other, axis=-1, keepdims=True)
    return q, kv, okv, own / total, other / total


def attend_kernel(scale, q_ref, kv_ref, okv_ref, info_ref, places_ref, out_ref):
    _, kv, okv, own, other = attention_parts(q_ref, kv_ref, okv_ref, info_ref, places_ref, scale)
    mixed = times(own.astype(bf16), kv[:, HD:]) + times(other.astype(bf16), okv[:, HD:])
    out_ref[0, :, 0] = mixed.astype(bf16).reshape(out_ref.shape[1], out_ref.shape[3], HD)


def attend_back_kernel(
    scale, q_ref, kv_ref, okv_ref, g_ref, info_ref, places_ref, gq_ref, gkv_ref, gokv_ref
):
    q, kv, okv, own, other = attention_parts(q_ref, kv_ref, okv_ref, info_ref, places_ref, scale)
    g = g_ref[0, :, 0].reshape(-1, HD)
    grad_own = times_transposed(g, kv[:, HD:])
    grad_other = times_transposed(g, okv[:, HD:])
    centre = jnp.sum(own * grad_own, axis=-1, keepdims=True) + jnp.sum(
        other * grad_other, axis=-1, keepdims=True
    )
    score_own = (own * (grad_own - centre)).astype(bf16)
    score_other = (other * (grad_other - centre)).astype(bf16)

    def put(ref, lanes, value):
        ref[0, :, 0, :, lanes] = value.astype(ref.dtype).reshape(ref.shape[1], ref.shape[3], HD)

    first, second = slice(0, HD), slice(HD, 2 * HD)
    put(gokv_ref, first, transposed_times(score_other, q) * scale)
    put(gokv_ref, second, transposed_times(other.astype(bf16), g))
    put(gkv_ref, first, transposed_times(score_own, q) * scale)
    put(gkv_ref, second, transposed_times(own.astype(bf16), g))
    put(gq_ref, first, (times(score_own, kv[:, :HD]) + times(score_other, okv[:, :HD])) * scale)


def attention_call(kernel, inputs, info, places, outputs):
    twins, pieces, rows, tok, width = inputs[0].shape
    heads = width // HD
    span = pieces * tok

    def block(array):
        return pl.BlockSpec(
            (1, pieces, 1, tok, array.shape[-1] // heads), lambda c, r, h: (c, 0, r, 0, h)
        )

    return pl.pallas_call(
        kernel,
        grid=(twins, rows, heads),
        in_specs=[block(a) for a in inputs]
        + [
            pl.BlockSpec((1, 1, span, 2), lambda c, r, h: (c, r, 0, 0)),
            pl.BlockSpec(places.shape, lambda c, r, h: (0, 0)),
        ],
        out_specs=[block(a) for a in outputs],
        out_shape=outputs,
        compiler_params=pltpu.CompilerParams(vmem_limit_bytes=48 * 1024 * 1024),
        cost_estimate=pl.CostEstimate(flops=1, bytes_accessed=1, transcendentals=0),
    )(*inputs, info, places)


def twins_kernel(sides_ref, kept_ref, given_ref, out_ref):
    out_ref[...] = add_low(kept_ref[...], given_ref[...])


def owner_kernel(unit, sides_ref, kept_ref, given_ref, twins_ref, *outs):
    mine = kept_ref[...].astype(f32) + given_ref[...].astype(f32)
    mine = jnp.where(sides_ref[0] == sides_ref[1], mine, twins_ref[...].astype(f32))
    if len(outs) == 1:
        outs[0][...] = mine
        return
    for i in range(mine.shape[1] // unit):
        j = i // 2 * unit
        outs[i % 2][:, j : j + unit] = mine[:, i * unit : (i + 1) * unit]


def halves_call(turned, kernel, sides, inputs, maps, outputs):
    rows = inputs[0].shape[1 if turned else 0] // 4

    def block(pick, array):
        if turned:
            return pl.BlockSpec((array.shape[0], rows), lambda i, s: (0, pick(i, s[0], s[1])))
        return pl.BlockSpec((rows, array.shape[1]), lambda i, s: (pick(i, s[0], s[1]), 0))

    return pl.pallas_call(
        kernel,
        grid_spec=pltpu.PrefetchScalarGridSpec(
            num_scalar_prefetch=1,
            grid=(2,),
            in_specs=[block(pick, a) for pick, a in zip(maps, inputs)],
            out_specs=[block(lambda i, z, t: i, a) for a in outputs],
        ),
        out_shape=outputs,
        cost_estimate=pl.CostEstimate(
            flops=0,
            bytes_accessed=sum(a.size * a.dtype.itemsize for a in [*inputs, *outputs]),
            transcendentals=0,
        ),
    )(sides, *inputs)


def split_kernel(unit, *refs):
    *sources, out = refs
    number = len(sources)
    for j in range(out.shape[0]):
        cols = out.shape[2] // number
        for i, source in enumerate(sources):
            for u in range(cols // unit):
                place = (u * number + i) * unit
                first = j * cols + u * unit
                out[j, :, place : place + unit] = source[:, first : first + unit]


def stack_kernel(*refs):
    *sources, out = refs
    rows, cols = sources[0].shape[0], out.shape[2]
    for i, source in enumerate(sources):
        for j in range(out.shape[0]):
            out[j, i * rows : (i + 1) * rows] = source[:, j * cols : (j + 1) * cols]


def turn_kernel(source, *outs):
    rows = source.shape[1] // len(outs)
    for i, out in enumerate(outs):
        blocks = source[:, i * rows : (i + 1) * rows]
        out[...] = blocks.reshape(-1, blocks.shape[-1]).T


def permuted(value, flags):
    low = value.shape[1] // 8
    blocks = [value[:, i * low : (i + 1) * low] for i in (0, 2, 1, 3, 4, 6, 5, 7)]
    for mask, flag in ((2, flags[0]), (4, flags[1])):
        blocks = [jnp.where(flag, blocks[j ^ mask], blocks[j]) for j in range(8)]
    return blocks


def restored(value, flags):
    low = value.shape[1] // 8
    blocks = [value[:, i * low : (i + 1) * low] for i in range(8)]
    for mask, flag in ((2, flags[0]), (4, flags[1])):
        blocks = [jnp.where(flag, blocks[j ^ mask], blocks[j]) for j in range(8)]
    return [blocks[i] for i in (0, 2, 1, 3, 4, 6, 5, 7)]


def move_kernel(how, me_ref, *refs):
    flags = [me_ref[0] == 1, me_ref[1] == 1]
    number = len(refs) // 2
    for source, target in zip(refs[:number], refs[number:]):
        low = source.shape[1] // 8
        for i, block in enumerate(how(source[...], flags)):
            target[:, i * low : (i + 1) * low] = block


def local_call(kernel, scalars, inputs, outputs):
    vmem = pl.BlockSpec(memory_space=pltpu.VMEM)
    size = sum(a.size * a.dtype.itemsize for a in [*inputs, *outputs])
    return pl.pallas_call(
        kernel,
        in_specs=[pl.BlockSpec(memory_space=pltpu.SMEM)] * len(scalars) + [vmem] * len(inputs),
        out_specs=[vmem] * len(outputs),
        out_shape=outputs,
        compiler_params=pltpu.CompilerParams(vmem_limit_bytes=48 * 1024 * 1024),
        cost_estimate=pl.CostEstimate(flops=0, bytes_accessed=size, transcendentals=0),
    )(*scalars, *inputs)


class Places:
    def __init__(self):
        self.count = lax.axis_size(AXES)
        self.me = lax.axis_index(AXES)
        self.group = lax.axis_size(GROUP)
        self.half_bit = self.group // 2
        self.twin_bit = self.group
        self.far_bit = 2 * self.group
        self.z = lax.axis_index("uh")
        self.x = lax.axis_index("dh")
        self.twin = lax.axis_index("dl")

    def swap(self, value, mask):
        return lax.ppermute(value, AXES, [(i, i ^ mask) for i in range(self.count)])

    def send(self, value, mask, chosen):
        return lax.ppermute(
            value, AXES, [(i, i ^ mask) for i in range(self.count) if chosen(i)]
        )


def after(value, *others):
    return lax.optimization_barrier((value, others))[0]


def near_weights(at, weights, unit, *others):
    rows, width = weights[0].shape
    number, cols = len(weights), width // at.group
    kernel = functools.partial(split_kernel, unit) if unit else stack_kernel
    shape = (at.group, rows, number * cols) if unit else (at.group, number * rows, cols)
    (blocks,) = local_call(kernel, [], weights, [jax.ShapeDtypeStruct(shape, bf16)])
    if others:
        blocks = after(blocks, *others)
    near = lax.all_to_all(blocks, GROUP, split_axis=0, concat_axis=0, tiled=True)
    if unit:
        return near.reshape(at.group * rows, number * cols)
    return local_call(
        turn_kernel,
        [],
        [near],
        [jax.ShapeDtypeStruct((cols, at.group * rows), bf16)] * number,
    )


def gather(at, value):
    return lax.all_gather(value, GROUP, axis=0, tiled=True)


def scatter(at, pairs, product=times_transposed, before=(), behind=()):
    def term(side):
        total = None
        for left, right in pairs:
            part = lax.dynamic_slice_in_dim(left, side * (left.shape[0] // 2), left.shape[0] // 2)
            part = product(part, right)
            total = part if total is None else total + part
        return total

    given = at.swap(term(1 - at.twin).astype(bf16), at.twin_bit)
    kept = (term(at.twin) + given.astype(f32)).astype(bf16)
    kept = kept.reshape(at.half_bit, -1, kept.shape[1])
    if before:
        kept = after(kept, *before)
    kept = lax.all_to_all(kept, INNER, split_axis=0, concat_axis=0, tiled=True)
    if behind:
        kept = after(kept, *behind)
    return jnp.sum(kept.astype(f32), axis=0)


class Gradient:
    def __init__(self, at, pairs, turned=False):
        self.at, self.turned = at, turned
        cut = pairs[0][0].shape[1] // 2
        self.first = [(left[:, :cut], right) for left, right in pairs]
        self.there = self.product([(left[:, cut:], right) for left, right in pairs]).astype(bf16)
        self.given = at.swap(self.there, at.far_bit)

    def product(self, pairs):
        if self.turned:
            ((left, right),) = pairs
            return transposed_times(right, left)
        terms = [transposed_times(left, right) for left, right in pairs]
        return terms[0] if len(terms) == 1 else jnp.concatenate(terms, axis=1)

    def away(self, i):
        return (i // self.at.half_bit) % 2 != (i // self.at.twin_bit) % 2

    def across(self, *others):
        self.here = self.product(self.first)
        kept = (self.here + self.given.astype(f32)).astype(bf16)
        self.kept = after(kept, *others) if others else kept
        self.back = self.at.send(self.kept, self.at.half_bit, self.away)

    def call(self, kernel, inputs, maps, widths, kind):
        sides = jnp.stack([self.at.z, self.at.twin]).astype(jnp.int32)
        span = self.kept.shape[1 if self.turned else 0] // 2
        outs = [
            jax.ShapeDtypeStruct((width, span) if self.turned else (span, width), kind)
            for width in widths
        ]
        return halves_call(self.turned, kernel, sides, inputs, maps, outs)

    def to_twin(self):
        (twins,) = self.call(
            twins_kernel,
            [self.kept, self.back],
            [lambda i, z, t: 2 * i + 1 - t, lambda i, z, t: 2 * (1 - i) + 1 - t],
            [self.kept.shape[0 if self.turned else 1]],
            bf16,
        )
        self.twins = self.at.send(twins, self.at.twin_bit, lambda i: not self.away(i))

    def finish(self, unit=None):
        cols = self.kept.shape[0 if self.turned else 1]
        outs = self.call(
            functools.partial(owner_kernel, unit),
            [self.kept, self.back, self.twins],
            [
                lambda i, z, t: 2 * (i ^ z) + t,
                lambda i, z, t: 2 * (1 - (i ^ z)) + t,
                lambda i, z, t: i ^ z,
            ],
            [cols // 2, cols // 2] if unit else [cols],
            f32,
        )
        return [out.T if self.turned else out for out in outs]


def reduce_gains(at, terms):
    number, width = terms.shape
    terms = terms.reshape(number, 2, 2, 2, -1)
    terms = jnp.where(at.x == 1, terms[:, ::-1], terms)
    terms = jnp.where(at.z == 1, terms[:, :, ::-1], terms)
    terms = terms.transpose(0, 1, 3, 2, 4).reshape(number, at.count, -1).transpose(1, 0, 2)
    terms = lax.all_to_all(terms, AXES, split_axis=0, concat_axis=0, tiled=True)
    return jnp.sum(terms, axis=0)


def on_device(
    tokens,
    memory,
    lengths,
    gain_attn,
    gain_memory,
    gain_ffn,
    w_query,
    w_key,
    w_value,
    w_out,
    w_gate,
    w_up,
    w_down,
    cotangent,
):
    at = Places()
    rows_here, tok_row, model_width = tokens.shape
    count = rows_here * tok_row
    group = at.group
    half = group // 2
    head_width = w_query.shape[1]
    own_width = head_width // group
    width = max(own_width, HD)
    scale = HD ** (-0.5)

    bounds = jnp.cumsum(lengths, axis=1)
    twin_bounds = at.swap(bounds, at.twin_bit)
    first = at.twin == 0
    all_bounds = jnp.stack(
        [jnp.where(first, bounds, twin_bounds), jnp.where(first, twin_bounds, bounds)]
    )
    span = half * tok_row
    places = jnp.arange(span, dtype=jnp.int32)
    own_places = at.z * span + places
    other_places = (1 - at.z) * span + places
    passed = all_bounds[:, :, None, :] <= own_places[None, None, :, None]
    starts = jnp.max(jnp.where(passed, all_bounds[:, :, None, :], 0), axis=-1)
    info = jnp.stack([starts, jnp.broadcast_to(own_places, starts.shape)], axis=-1)
    key_places = jnp.stack([own_places, other_places])
    position = at.me % group
    here = position * tok_row + jnp.arange(tok_row, dtype=jnp.int32)
    valid = (here[None] < bounds[:, -1:]).astype(f32).reshape(count, 1)

    unit = min(own_width, HD)
    cache_near = near_weights(at, [w_key, w_value], unit)
    query_near = near_weights(at, [w_query, w_out], own_width, cache_near)
    sides = jnp.stack([at.z, at.x]).astype(jnp.int32)
    entry = [a.reshape(count, model_width) for a in (memory, tokens, cotangent)] + [
        gain.reshape(1, model_width) for gain in (gain_attn, gain_memory, gain_ffn)
    ]
    memory, tokens, cotangent, gain_attn, gain_memory, gain_ffn = local_call(
        functools.partial(move_kernel, permuted),
        [sides],
        entry,
        [jax.ShapeDtypeStruct(a.shape, a.dtype) for a in entry],
    )
    residual_in = tokens.astype(f32)
    token_normed, token_inverse = normalize(residual_in)
    token_in = (token_normed * gain_attn).astype(bf16)
    memory_normed, memory_inverse = normalize(memory.astype(f32))
    memory_in = (memory_normed * gain_memory).astype(bf16)
    grad_final = cotangent.astype(f32) * valid

    parts = HD // own_width if own_width < HD else 1

    def widen(value):
        if parts == 1:
            return value
        assert parts == lax.axis_size("blk")
        return lax.all_gather(value, "blk", axis=1, tiled=True)

    def narrow(value):
        if parts == 1:
            return value
        return lax.dynamic_slice_in_dim(
            value, lax.axis_index("blk") * own_width, own_width, axis=1
        )

    def heads(value):
        return value.reshape(2, half, rows_here, tok_row, -1)

    memory_all = gather(at, after(memory_in, cache_near))
    cache_half = at.swap(cache_near, at.half_bit)
    cache_far = at.swap(cache_near, at.far_bit)
    cache_far_half = at.swap(cache_half, at.far_bit)
    cache_w = jnp.concatenate([cache_near, cache_half, cache_far, cache_far_half], axis=0)
    memory_all = after(memory_all, cache_half, cache_far, query_near, info)
    query_later = after(query_near, cache_half)
    query_half = at.swap(query_later, at.half_bit)
    query_far = at.swap(query_later, at.far_bit)
    token_all = gather(at, after(token_in, memory_all))
    memory_all = after(memory_all, query_half, query_far, cache_w)

    def first_half(i):
        return (i // at.half_bit) % 2 == 0

    def second_half(i):
        return not first_half(i)

    cache = times(memory_all, cache_w, bf16)
    if parts > 1:
        cache = jnp.concatenate(
            [widen(cache[:, :own_width]), widen(cache[:, own_width:])], axis=1
        )
    cache = heads(cache)
    other_cache = at.send(cache, at.half_bit, first_half)
    token_all = after(token_all, other_cache)
    query_far_half = at.swap(after(query_half, cache), at.far_bit)
    query_parts = [query_near, query_half, query_far, query_far_half]
    query_w = jnp.concatenate([part[:, :own_width] for part in query_parts], axis=0)
    out_w = jnp.concatenate([part[:, own_width:] for part in query_parts], axis=0)
    queries = heads(widen(times(token_all, query_w, bf16)))
    gate_near, up_near, down_near = near_weights(
        at, [w_gate, w_up, w_down], None, query_near, cache
    )
    (mixed,) = attention_call(
        functools.partial(attend_kernel, scale),
        [after(queries, gate_near), cache, other_cache],
        info,
        key_places,
        [queries],
    )
    gate_far, up_far, down_far = (
        at.swap(near, at.far_bit) for near in (gate_near, up_near, down_near)
    )
    mixed = narrow(mixed.reshape(group * count, width))
    mixed = after(mixed, gate_far)
    gate_half = at.swap(after(gate_near, other_cache), at.half_bit)

    def whole(near, half_part, far_part, far_half_part):
        return jnp.concatenate([near, half_part, far_part, far_half_part], axis=1)

    residual = residual_in + scatter(
        at, [(mixed, out_w)], times_transposed, (gate_half,), (up_far,)
    )
    ffn_normed, ffn_inverse = normalize(residual)
    ffn_in = (ffn_normed * gain_ffn).astype(bf16)
    up_half = at.swap(after(up_near, gate_half), at.half_bit)
    gate_w = whole(gate_near, gate_half, gate_far, at.swap(gate_half, at.far_bit))
    ffn_all = after(gather(at, ffn_in), up_half, down_far, gate_w)
    final_all = gather(at, after(grad_final.astype(bf16), ffn_all))
    down_half = at.swap(after(down_near, up_half), at.half_bit)
    gate = times_transposed(ffn_all, gate_w)
    up_w = whole(up_near, up_half, up_far, at.swap(up_half, at.far_bit))
    up = times_transposed(ffn_all, after(up_w, gate))
    down_w = whole(
        down_near, after(down_half, up), down_far, at.swap(down_half, at.far_bit)
    )
    grad_hidden = times_transposed(final_all, down_w)
    gate_sigmoid = jax.nn.sigmoid(gate)
    silu = gate * gate_sigmoid
    hidden = (silu * up).astype(bf16)
    grad_gate_in = (
        grad_hidden * up * gate_sigmoid * (1.0 + gate * (1.0 - gate_sigmoid))
    ).astype(bf16)
    grad_up_in = (grad_hidden * silu).astype(bf16)
    gate_grad = Gradient(at, [(ffn_all, grad_gate_in)], True)
    up_grad = Gradient(at, [(ffn_all, grad_up_in)], True)
    grad_ffn_in = scatter(
        at,
        [(after(grad_gate_in, gate_grad.there), gate_w), (grad_up_in, up_w)],
        times,
        (),
        (up_grad.there,),
    )
    grad_residual = grad_final + norm_back(grad_ffn_in, ffn_normed, ffn_inverse, gain_ffn)
    gain_ffn_term = jnp.sum(grad_ffn_in * ffn_normed, axis=0)
    grad_branch = grad_residual.astype(bf16)
    hidden = after(hidden, grad_branch)
    down_grad = Gradient(at, [(final_all, hidden)], True)
    branch_all = gather(at, after(grad_branch, gate_grad.given))
    gate_grad.across(grad_branch)
    up_grad.across()
    gathered = branch_all
    branch_all = after(branch_all, gate_grad.kept, up_grad.kept)
    grad_mixed = heads(widen(times(branch_all, out_w, bf16)))
    grad_queries, grad_cache, grad_other_cache = attention_call(
        functools.partial(attend_back_kernel, scale),
        [queries, cache, other_cache, after(grad_mixed, gate_grad.back)],
        info,
        key_places,
        [
            queries,
            jax.ShapeDtypeStruct(cache.shape, f32),
            cache,
        ],
    )
    given_cache = at.send(grad_other_cache, at.half_bit, second_half)
    grad_queries = narrow(grad_queries.reshape(group * count, width))
    output = residual + scatter(at, [(hidden, down_w)], times, (gathered,))
    gate_grad.to_twin()
    (gate_out,) = gate_grad.finish()
    query_grad = Gradient(at, [(token_all, grad_queries), (branch_all, mixed)])

    grad_token_in = scatter(at, [(grad_queries, query_w)])
    given_cache = after(given_cache, gate_out, up_grad.back, query_grad.there, down_grad.given)
    down_grad.across(given_cache)
    up_grad.to_twin()
    grad_cache = (grad_cache + given_cache.astype(f32)).astype(bf16)
    grad_cache = grad_cache.reshape(group * count, 2 * width)
    if parts > 1:
        grad_cache = jnp.concatenate(
            [narrow(grad_cache[:, :width]), narrow(grad_cache[:, width:])], axis=1
        )
    cache_grad = Gradient(at, [(memory_all, grad_cache)])
    query_grad.across(down_grad.back)
    cache_grad.across(down_grad.back)
    grad_memory_in = scatter(
        at,
        [(after(grad_cache, cache_grad.there), cache_w)],
        times_transposed,
        (),
        (query_grad.back, up_grad.twins),
    )
    for grad in (down_grad, query_grad, cache_grad):
        grad.to_twin()
    (up_out,), (down_out,) = (grad.finish() for grad in (up_grad, down_grad))
    query_out, out_out = query_grad.finish(own_width)
    key_out, value_out = cache_grad.finish(unit)

    cut = model_width // 2
    gain_memory_term = (
        jnp.concatenate(
            [
                jnp.sum(cache_grad.here * cache_w[:cut].astype(f32), axis=1),
                jnp.sum(cache_grad.there.astype(f32) * cache_w[cut:].astype(f32), axis=1),
            ]
        )
        / gain_memory[0]
    )
    gain_attn_term = jnp.sum(grad_token_in * token_normed, axis=0)
    gain_grads = reduce_gains(at, jnp.stack([gain_attn_term, gain_memory_term, gain_ffn_term]))

    grad_tokens = grad_residual + norm_back(grad_token_in, token_normed, token_inverse, gain_attn)
    grad_memory = norm_back(grad_memory_in, memory_normed, memory_inverse, gain_memory)
    leaving = [a.astype(bf16) for a in (output, grad_tokens, grad_memory)]
    leaving = local_call(
        functools.partial(move_kernel, restored),
        [sides],
        leaving,
        [jax.ShapeDtypeStruct(a.shape, a.dtype) for a in leaving],
    )
    output, grad_tokens, grad_memory = (
        a.reshape(rows_here, tok_row, model_width) for a in leaving
    )
    return (
        output,
        grad_tokens,
        grad_memory,
        gain_grads[0],
        gain_grads[1],
        gain_grads[2],
        query_out,
        key_out,
        value_out,
        out_out,
        gate_out,
        up_out,
        down_out,
    )


def solution(mesh):
    dp, ulysses, blk = (mesh.shape[axis] for axis in ("dp", "ulysses", "blk"))
    mesh = jax.sharding.Mesh(mesh.devices.reshape(dp // 2, 2, 2, ulysses // 2, blk), AXES)
    dp, places = ("dh", "dl"), ("uh", "ul", "blk")
    rows = P(dp, places, None)
    weight = P(AXES, None)
    grad = P(dp, places)
    return jax.shard_map(
        on_device,
        mesh=mesh,
        in_specs=(rows, rows, P(dp, None), P(), P(), P()) + (weight,) * 7 + (rows,),
        out_specs=(rows,) * 3 + (P(AXES),) * 3 + (grad,) * 7,
        check_vma=False,
    )
```

```python
import functools

import jax
import jax.numpy as jnp
from jax import lax
from jax.experimental import pallas as pl
from jax.experimental.pallas import tpu as pltpu
from jax.sharding import PartitionSpec as P

H = 16
HD = 128
AXES = ("dh", "dl", "uh", "ul", "blk")
GROUP = ("dl", "ul", "blk")
INNER = ("ul", "blk")
bf16 = jnp.bfloat16
f32 = jnp.float32
epsilon = 1e-06
negative = -1e30


def dot(left, right, over, kind=f32):
    return lax.dot_general(left, right, (over, ((), ())), preferred_element_type=kind)


def times(left, right, kind=f32):
    return dot(left, right, ((1,), (0,)), kind)


def times_transposed(left, right, kind=f32):
    return dot(left, right, ((1,), (1,)), kind)


def transposed_times(left, right, kind=f32):
    return dot(left, right, ((0,), (0,)), kind)


def normalize(values):
    inverse = lax.rsqrt(jnp.mean(values * values, axis=-1, keepdims=True) + epsilon)
    return (values * inverse, inverse)


def norm_back(grad_normed, normed, inverse, gain):
    scaled = grad_normed * gain
    return inverse * (scaled - normed * jnp.mean(scaled * normed, axis=-1, keepdims=True))


def add_low(left, right):
    return (left.astype(f32) + right.astype(f32)).astype(bf16)


def masked_scores(q, k, start, place, key_place, scale):
    scores = times_transposed(q, k) * scale
    allowed = (key_place >= start) & (key_place <= place)
    return jnp.where(allowed, scores, negative)


def attention_parts(q_ref, kv_ref, okv_ref, info_ref, places_ref, scale):
    q = q_ref[0, :, 0].reshape(-1, HD)
    kv = kv_ref[0, :, 0].reshape(-1, 2 * HD)
    okv = okv_ref[0, :, 0].reshape(-1, 2 * HD)
    start = info_ref[0, 0, :, 0:1]
    place = info_ref[0, 0, :, 1:2]
    own = masked_scores(q, kv[:, :HD], start, place, places_ref[0:1, :], scale)
    other = masked_scores(q, okv[:, :HD], start, place, places_ref[1:2, :], scale)
    largest = jnp.maximum(
        jnp.max(own, axis=-1, keepdims=True), jnp.max(other, axis=-1, keepdims=True)
    )
    own = jnp.exp(own - largest)
    other = jnp.exp(other - largest)
    total = jnp.sum(own, axis=-1, keepdims=True) + jnp.sum(other, axis=-1, keepdims=True)
    return q, kv, okv, own / total, other / total


def attend_kernel(scale, q_ref, kv_ref, okv_ref, info_ref, places_ref, out_ref):
    _, kv, okv, own, other = attention_parts(q_ref, kv_ref, okv_ref, info_ref, places_ref, scale)
    mixed = times(own.astype(bf16), kv[:, HD:]) + times(other.astype(bf16), okv[:, HD:])
    out_ref[0, :, 0] = mixed.astype(bf16).reshape(out_ref.shape[1], out_ref.shape[3], HD)


def attend_back_kernel(
    scale, q_ref, kv_ref, okv_ref, g_ref, info_ref, places_ref, gq_ref, gkv_ref, gokv_ref
):
    q, kv, okv, own, other = attention_parts(q_ref, kv_ref, okv_ref, info_ref, places_ref, scale)
    g = g_ref[0, :, 0].reshape(-1, HD)
    grad_own = times_transposed(g, kv[:, HD:])
    grad_other = times_transposed(g, okv[:, HD:])
    centre = jnp.sum(own * grad_own, axis=-1, keepdims=True) + jnp.sum(
        other * grad_other, axis=-1, keepdims=True
    )
    score_own = (own * (grad_own - centre)).astype(bf16)
    score_other = (other * (grad_other - centre)).astype(bf16)

    def put(ref, lanes, value):
        ref[0, :, 0, :, lanes] = value.astype(ref.dtype).reshape(ref.shape[1], ref.shape[3], HD)

    first, second = slice(0, HD), slice(HD, 2 * HD)
    put(gokv_ref, first, transposed_times(score_other, q) * scale)
    put(gokv_ref, second, transposed_times(other.astype(bf16), g))
    put(gkv_ref, first, transposed_times(score_own, q) * scale)
    put(gkv_ref, second, transposed_times(own.astype(bf16), g))
    put(gq_ref, first, (times(score_own, kv[:, :HD]) + times(score_other, okv[:, :HD])) * scale)


def attention_call(kernel, inputs, info, places, outputs):
    twins, pieces, rows, tok, width = inputs[0].shape
    heads = width // HD
    span = pieces * tok

    def block(array):
        return pl.BlockSpec(
            (1, pieces, 1, tok, array.shape[-1] // heads), lambda c, r, h: (c, 0, r, 0, h)
        )

    return pl.pallas_call(
        kernel,
        grid=(twins, rows, heads),
        in_specs=[block(a) for a in inputs]
        + [
            pl.BlockSpec((1, 1, span, 2), lambda c, r, h: (c, r, 0, 0)),
            pl.BlockSpec(places.shape, lambda c, r, h: (0, 0)),
        ],
        out_specs=[block(a) for a in outputs],
        out_shape=outputs,
        compiler_params=pltpu.CompilerParams(vmem_limit_bytes=48 * 1024 * 1024),
        cost_estimate=pl.CostEstimate(flops=1, bytes_accessed=1, transcendentals=0),
    )(*inputs, info, places)


def twins_kernel(sides_ref, kept_ref, given_ref, out_ref):
    out_ref[...] = add_low(kept_ref[...], given_ref[...])


def owner_kernel(unit, sides_ref, kept_ref, given_ref, twins_ref, *outs):
    mine = kept_ref[...].astype(f32) + given_ref[...].astype(f32)
    mine = jnp.where(sides_ref[0] == sides_ref[1], mine, twins_ref[...].astype(f32))
    if len(outs) == 1:
        outs[0][...] = mine
        return
    for i in range(mine.shape[1] // unit):
        j = i // 2 * unit
        outs[i % 2][:, j : j + unit] = mine[:, i * unit : (i + 1) * unit]


def halves_call(turned, kernel, sides, inputs, maps, outputs):
    rows = inputs[0].shape[1 if turned else 0] // 4

    def block(pick, array):
        if turned:
            return pl.BlockSpec((array.shape[0], rows), lambda i, s: (0, pick(i, s[0], s[1])))
        return pl.BlockSpec((rows, array.shape[1]), lambda i, s: (pick(i, s[0], s[1]), 0))

    return pl.pallas_call(
        kernel,
        grid_spec=pltpu.PrefetchScalarGridSpec(
            num_scalar_prefetch=1,
            grid=(2,),
            in_specs=[block(pick, a) for pick, a in zip(maps, inputs)],
            out_specs=[block(lambda i, z, t: i, a) for a in outputs],
        ),
        out_shape=outputs,
        cost_estimate=pl.CostEstimate(
            flops=0,
            bytes_accessed=sum(a.size * a.dtype.itemsize for a in [*inputs, *outputs]),
            transcendentals=0,
        ),
    )(sides, *inputs)


def split_kernel(unit, *refs):
    *sources, out = refs
    number = len(sources)
    for j in range(out.shape[0]):
        cols = out.shape[2] // number
        for i, source in enumerate(sources):
            for u in range(cols // unit):
                place = (u * number + i) * unit
                first = j * cols + u * unit
                out[j, :, place : place + unit] = source[:, first : first + unit]


def stack_kernel(*refs):
    *sources, out = refs
    rows, cols = sources[0].shape[0], out.shape[2]
    for i, source in enumerate(sources):
        for j in range(out.shape[0]):
            out[j, i * rows : (i + 1) * rows] = source[:, j * cols : (j + 1) * cols]


def turn_kernel(source, *outs):
    rows = source.shape[1] // len(outs)
    for i, out in enumerate(outs):
        blocks = source[:, i * rows : (i + 1) * rows]
        out[...] = blocks.reshape(-1, blocks.shape[-1]).T


def permuted(value, flags):
    low = value.shape[1] // 8
    blocks = [value[:, i * low : (i + 1) * low] for i in (0, 2, 1, 3, 4, 6, 5, 7)]
    for mask, flag in ((2, flags[0]), (4, flags[1])):
        blocks = [jnp.where(flag, blocks[j ^ mask], blocks[j]) for j in range(8)]
    return blocks


def restored(value, flags):
    low = value.shape[1] // 8
    blocks = [value[:, i * low : (i + 1) * low] for i in range(8)]
    for mask, flag in ((2, flags[0]), (4, flags[1])):
        blocks = [jnp.where(flag, blocks[j ^ mask], blocks[j]) for j in range(8)]
    return [blocks[i] for i in (0, 2, 1, 3, 4, 6, 5, 7)]


def move_kernel(how, me_ref, *refs):
    flags = [me_ref[0] == 1, me_ref[1] == 1]
    number = len(refs) // 2
    for source, target in zip(refs[:number], refs[number:]):
        low = source.shape[1] // 8
        for i, block in enumerate(how(source[...], flags)):
            target[:, i * low : (i + 1) * low] = block


def local_call(kernel, scalars, inputs, outputs):
    vmem = pl.BlockSpec(memory_space=pltpu.VMEM)
    size = sum(a.size * a.dtype.itemsize for a in [*inputs, *outputs])
    return pl.pallas_call(
        kernel,
        in_specs=[pl.BlockSpec(memory_space=pltpu.SMEM)] * len(scalars) + [vmem] * len(inputs),
        out_specs=[vmem] * len(outputs),
        out_shape=outputs,
        compiler_params=pltpu.CompilerParams(vmem_limit_bytes=48 * 1024 * 1024),
        cost_estimate=pl.CostEstimate(flops=0, bytes_accessed=size, transcendentals=0),
    )(*scalars, *inputs)


class Places:
    def __init__(self):
        self.count = lax.axis_size(AXES)
        self.me = lax.axis_index(AXES)
        self.group = lax.axis_size(GROUP)
        self.half_bit = self.group // 2
        self.twin_bit = self.group
        self.far_bit = 2 * self.group
        self.z = lax.axis_index("uh")
        self.x = lax.axis_index("dh")
        self.twin = lax.axis_index("dl")

    def swap(self, value, mask):
        return lax.ppermute(value, AXES, [(i, i ^ mask) for i in range(self.count)])

    def send(self, value, mask, chosen):
        return lax.ppermute(
            value, AXES, [(i, i ^ mask) for i in range(self.count) if chosen(i)]
        )


def after(value, *others):
    return lax.optimization_barrier((value, others))[0]


def near_weights(at, weights, unit, *others):
    rows, width = weights[0].shape
    number, cols = len(weights), width // at.group
    kernel = functools.partial(split_kernel, unit) if unit else stack_kernel
    shape = (at.group, rows, number * cols) if unit else (at.group, number * rows, cols)
    (blocks,) = local_call(kernel, [], weights, [jax.ShapeDtypeStruct(shape, bf16)])
    if others:
        blocks = after(blocks, *others)
    near = lax.all_to_all(blocks, GROUP, split_axis=0, concat_axis=0, tiled=True)
    if unit:
        return near.reshape(at.group * rows, number * cols)
    return local_call(
        turn_kernel,
        [],
        [near],
        [jax.ShapeDtypeStruct((cols, at.group * rows), bf16)] * number,
    )


def gather(at, value):
    return lax.all_gather(value, GROUP, axis=0, tiled=True)


def scatter(at, pairs, product=times_transposed, before=(), behind=()):
    def term(side):
        total = None
        for left, right in pairs:
            part = lax.dynamic_slice_in_dim(left, side * (left.shape[0] // 2), left.shape[0] // 2)
            part = product(part, right)
            total = part if total is None else total + part
        return total

    given = at.swap(term(1 - at.twin).astype(bf16), at.twin_bit)
    kept = (term(at.twin) + given.astype(f32)).astype(bf16)
    kept = kept.reshape(at.half_bit, -1, kept.shape[1])
    if before:
        kept = after(kept, *before)
    at.kept = kept
    kept = lax.all_to_all(kept, INNER, split_axis=0, concat_axis=0, tiled=True)
    if behind:
        kept = after(kept, *behind)
    return jnp.sum(kept.astype(f32), axis=0)


class Gradient:
    def __init__(self, at, pairs, turned=False):
        self.at, self.turned = at, turned
        cut = pairs[0][0].shape[1] // 2
        self.first = [(left[:, :cut], right) for left, right in pairs]
        self.there = self.product([(left[:, cut:], right) for left, right in pairs]).astype(bf16)
        self.given = at.swap(self.there, at.far_bit)

    def product(self, pairs):
        if self.turned:
            ((left, right),) = pairs
            return transposed_times(right, left)
        terms = [transposed_times(left, right) for left, right in pairs]
        return terms[0] if len(terms) == 1 else jnp.concatenate(terms, axis=1)

    def away(self, i):
        return (i // self.at.half_bit) % 2 != (i // self.at.twin_bit) % 2

    def across(self, *others):
        self.here = self.product(self.first)
        kept = (self.here + self.given.astype(f32)).astype(bf16)
        self.kept = after(kept, *others) if others else kept
        self.back = self.at.send(self.kept, self.at.half_bit, self.away)

    def call(self, kernel, inputs, maps, widths, kind):
        sides = jnp.stack([self.at.z, self.at.twin]).astype(jnp.int32)
        span = self.kept.shape[1 if self.turned else 0] // 2
        outs = [
            jax.ShapeDtypeStruct((width, span) if self.turned else (span, width), kind)
            for width in widths
        ]
        return halves_call(self.turned, kernel, sides, inputs, maps, outs)

    def to_twin(self):
        (twins,) = self.call(
            twins_kernel,
            [self.kept, self.back],
            [lambda i, z, t: 2 * i + 1 - t, lambda i, z, t: 2 * (1 - i) + 1 - t],
            [self.kept.shape[0 if self.turned else 1]],
            bf16,
        )
        self.twins = self.at.send(twins, self.at.twin_bit, lambda i: not self.away(i))

    def finish(self, unit=None):
        cols = self.kept.shape[0 if self.turned else 1]
        outs = self.call(
            functools.partial(owner_kernel, unit),
            [self.kept, self.back, self.twins],
            [
                lambda i, z, t: 2 * (i ^ z) + t,
                lambda i, z, t: 2 * (1 - (i ^ z)) + t,
                lambda i, z, t: i ^ z,
            ],
            [cols // 2, cols // 2] if unit else [cols],
            f32,
        )
        return [out.T if self.turned else out for out in outs]


def reduce_gains(at, terms):
    number, width = terms.shape
    terms = terms.reshape(number, 2, 2, 2, -1)
    terms = jnp.where(at.x == 1, terms[:, ::-1], terms)
    terms = jnp.where(at.z == 1, terms[:, :, ::-1], terms)
    terms = terms.transpose(0, 1, 3, 2, 4).reshape(number, at.count, -1).transpose(1, 0, 2)
    terms = lax.all_to_all(terms, AXES, split_axis=0, concat_axis=0, tiled=True)
    return jnp.sum(terms, axis=0)


def on_device(
    tokens,
    memory,
    lengths,
    gain_attn,
    gain_memory,
    gain_ffn,
    w_query,
    w_key,
    w_value,
    w_out,
    w_gate,
    w_up,
    w_down,
    cotangent,
):
    at = Places()
    rows_here, tok_row, model_width = tokens.shape
    count = rows_here * tok_row
    group = at.group
    half = group // 2
    head_width = w_query.shape[1]
    own_width = head_width // group
    width = max(own_width, HD)
    scale = HD ** (-0.5)

    bounds = jnp.cumsum(lengths, axis=1)
    twin_bounds = at.swap(bounds, at.twin_bit)
    first = at.twin == 0
    all_bounds = jnp.stack(
        [jnp.where(first, bounds, twin_bounds), jnp.where(first, twin_bounds, bounds)]
    )
    span = half * tok_row
    places = jnp.arange(span, dtype=jnp.int32)
    own_places = at.z * span + places
    other_places = (1 - at.z) * span + places
    passed = all_bounds[:, :, None, :] <= own_places[None, None, :, None]
    starts = jnp.max(jnp.where(passed, all_bounds[:, :, None, :], 0), axis=-1)
    info = jnp.stack([starts, jnp.broadcast_to(own_places, starts.shape)], axis=-1)
    key_places = jnp.stack([own_places, other_places])
    position = at.me % group
    here = position * tok_row + jnp.arange(tok_row, dtype=jnp.int32)
    valid = (here[None] < bounds[:, -1:]).astype(f32).reshape(count, 1)

    unit = min(own_width, HD)
    cache_near = near_weights(at, [w_key, w_value], unit)
    query_near = near_weights(at, [w_query, w_out], own_width, cache_near)
    sides = jnp.stack([at.z, at.x]).astype(jnp.int32)
    entry = [a.reshape(count, model_width) for a in (memory, tokens, cotangent)] + [
        gain.reshape(1, model_width) for gain in (gain_attn, gain_memory, gain_ffn)
    ]
    memory, tokens, cotangent, gain_attn, gain_memory, gain_ffn = local_call(
        functools.partial(move_kernel, permuted),
        [sides],
        entry,
        [jax.ShapeDtypeStruct(a.shape, a.dtype) for a in entry],
    )
    residual_in = tokens.astype(f32)
    token_normed, token_inverse = normalize(residual_in)
    token_in = (token_normed * gain_attn).astype(bf16)
    memory_normed, memory_inverse = normalize(memory.astype(f32))
    memory_in = (memory_normed * gain_memory).astype(bf16)
    grad_final = cotangent.astype(f32) * valid

    parts = HD // own_width if own_width < HD else 1

    def widen(value):
        if parts == 1:
            return value
        assert parts == lax.axis_size("blk")
        return lax.all_gather(value, "blk", axis=1, tiled=True)

    def narrow(value):
        if parts == 1:
            return value
        return lax.dynamic_slice_in_dim(
            value, lax.axis_index("blk") * own_width, own_width, axis=1
        )

    def heads(value):
        return value.reshape(2, half, rows_here, tok_row, -1)

    memory_all = gather(at, after(memory_in, cache_near))
    cache_half = at.swap(cache_near, at.half_bit)
    cache_far = at.swap(cache_near, at.far_bit)
    cache_far_half = at.swap(cache_half, at.far_bit)
    cache_w = jnp.concatenate([cache_near, cache_half, cache_far, cache_far_half], axis=0)
    memory_all = after(memory_all, cache_half, cache_far, query_near, info)
    query_later = after(query_near, cache_half)
    query_half = at.swap(query_later, at.half_bit)
    query_far = at.swap(query_later, at.far_bit)
    token_all = gather(at, after(token_in, memory_all))
    memory_all = after(memory_all, query_half, query_far, cache_w)

    def first_half(i):
        return (i // at.half_bit) % 2 == 0

    def second_half(i):
        return not first_half(i)

    cache = times(memory_all, cache_w, bf16)
    if parts > 1:
        cache = jnp.concatenate(
            [widen(cache[:, :own_width]), widen(cache[:, own_width:])], axis=1
        )
    cache = heads(cache)
    other_cache = at.send(cache, at.half_bit, first_half)
    gathered_tokens = token_all
    token_all = after(token_all, other_cache)
    query_far_half = at.swap(after(query_half, cache), at.far_bit)
    query_parts = [query_near, query_half, query_far, query_far_half]
    query_w = jnp.concatenate([part[:, :own_width] for part in query_parts], axis=0)
    out_w = jnp.concatenate([part[:, own_width:] for part in query_parts], axis=0)
    queries = heads(widen(times(token_all, query_w, bf16)))
    gate_near, up_near, down_near = near_weights(
        at, [w_gate, w_up, w_down], None, gathered_tokens, cache
    )
    (mixed,) = attention_call(
        functools.partial(attend_kernel, scale),
        [after(queries, gate_near), cache, other_cache],
        info,
        key_places,
        [queries],
    )
    gate_far, up_far, down_far = (
        at.swap(near, at.far_bit) for near in (gate_near, up_near, down_near)
    )
    mixed = narrow(mixed.reshape(group * count, width))
    mixed = after(mixed, gate_far)
    gate_half = at.swap(after(gate_near, other_cache), at.half_bit)

    def whole(near, half_part, far_part, far_half_part):
        return jnp.concatenate([near, half_part, far_part, far_half_part], axis=1)

    up_half = at.swap(after(up_near, gate_half), at.half_bit)
    residual = residual_in + scatter(
        at, [(mixed, out_w)], times_transposed, (gate_half,), (up_half, up_far)
    )
    ffn_normed, ffn_inverse = normalize(residual)
    ffn_in = (ffn_normed * gain_ffn).astype(bf16)
    down_half = at.swap(after(down_near, up_half), at.half_bit)
    gate_w = whole(gate_near, gate_half, gate_far, at.swap(gate_half, at.far_bit))
    up_w = whole(up_near, up_half, up_far, at.swap(up_half, at.far_bit))
    ffn_all = after(gather(at, ffn_in), down_half, down_far, gate_w, up_w)
    final_all = gather(at, after(grad_final.astype(bf16), other_cache))
    gate = times_transposed(ffn_all, gate_w)
    up = times_transposed(ffn_all, after(up_w, gate))
    down_w = whole(
        down_near, after(down_half, up), down_far, at.swap(down_half, at.far_bit)
    )
    grad_hidden = times_transposed(final_all, down_w)
    gate_sigmoid = jax.nn.sigmoid(gate)
    silu = gate * gate_sigmoid
    hidden = (silu * up).astype(bf16)
    grad_gate_in = (
        grad_hidden * up * gate_sigmoid * (1.0 + gate * (1.0 - gate_sigmoid))
    ).astype(bf16)
    grad_up_in = (grad_hidden * silu).astype(bf16)
    gate_grad = Gradient(at, [(ffn_all, grad_gate_in)], True)
    up_grad = Gradient(at, [(ffn_all, grad_up_in)], True)
    grad_ffn_in = scatter(
        at,
        [(after(grad_gate_in, gate_grad.there), gate_w), (grad_up_in, up_w)],
        times,
        (),
        (up_grad.there,),
    )
    grad_residual = grad_final + norm_back(grad_ffn_in, ffn_normed, ffn_inverse, gain_ffn)
    gain_ffn_term = jnp.sum(grad_ffn_in * ffn_normed, axis=0)
    grad_branch = grad_residual.astype(bf16)
    hidden = after(hidden, grad_branch)
    down_grad = Gradient(at, [(final_all, hidden)], True)
    branch_all = gather(at, after(grad_branch, gate_grad.given))
    gate_grad.across(grad_branch)
    up_grad.across()
    gathered = branch_all
    branch_all = after(branch_all, gate_grad.kept, up_grad.kept)
    grad_mixed = heads(widen(times(branch_all, out_w, bf16)))
    grad_queries, grad_cache, grad_other_cache = attention_call(
        functools.partial(attend_back_kernel, scale),
        [queries, cache, other_cache, grad_mixed],
        info,
        key_places,
        [
            queries,
            jax.ShapeDtypeStruct(cache.shape, f32),
            cache,
        ],
    )
    given_cache = at.send(grad_other_cache, at.half_bit, second_half)
    grad_queries = narrow(grad_queries.reshape(group * count, width))
    grad_token_in = scatter(at, [(grad_queries, query_w)])
    gate_grad.to_twin()
    (gate_out,) = gate_grad.finish()
    query_grad = Gradient(at, [(token_all, grad_queries), (branch_all, mixed)])

    given_cache = after(
        given_cache, gate_out, up_grad.back, query_grad.given, down_grad.given
    )
    up_grad.to_twin()
    grad_cache = (grad_cache + given_cache.astype(f32)).astype(bf16)
    grad_cache = grad_cache.reshape(group * count, 2 * width)
    if parts > 1:
        grad_cache = jnp.concatenate(
            [narrow(grad_cache[:, :width]), narrow(grad_cache[:, width:])], axis=1
        )
    cache_grad = Gradient(at, [(memory_all, grad_cache)])
    down_grad.across(grad_cache)
    before = (cache_grad.given, down_grad.back)
    cache_grad.across()
    grad_memory_in = scatter(
        at,
        [(after(grad_cache, cache_grad.there, down_grad.kept), cache_w)],
        times_transposed,
        before,
        (up_grad.twins,),
    )
    query_grad.across(cache_grad.kept)
    down_grad.to_twin()
    (up_out,) = up_grad.finish()
    cache_grad.to_twin()
    cut = model_width // 2
    gain_memory_term = (
        jnp.concatenate(
            [
                jnp.sum(cache_grad.here * cache_w[:cut].astype(f32), axis=1),
                jnp.sum(cache_grad.there.astype(f32) * cache_w[cut:].astype(f32), axis=1),
            ]
        )
        / gain_memory[0]
    )
    gain_attn_term = jnp.sum(grad_token_in * token_normed, axis=0)
    gain_terms = jnp.stack([gain_attn_term, gain_memory_term, gain_ffn_term])
    gain_grads = reduce_gains(at, gain_terms)

    def left(value):
        value = value.astype(bf16)
        (value,) = local_call(
            functools.partial(move_kernel, restored),
            [sides],
            [value],
            [jax.ShapeDtypeStruct(value.shape, value.dtype)],
        )
        return value

    output_term = scatter(
        at,
        [(after(hidden, at.kept, cache_grad.kept), down_w)],
        times,
        (cache_grad.back, gain_grads),
        (query_grad.back, cache_grad.twins, up_out, down_grad.twins),
    )
    grad_tokens = left(
        grad_residual + norm_back(grad_token_in, token_normed, token_inverse, gain_attn)
    )
    grad_memory = left(norm_back(grad_memory_in, memory_normed, memory_inverse, gain_memory))
    output = left(residual + output_term)
    leaving = [output, grad_tokens, grad_memory]
    query_grad.to_twin()
    (down_out,) = down_grad.finish()
    query_out, out_out = query_grad.finish(own_width)
    key_out, value_out = cache_grad.finish(unit)
    output, grad_tokens, grad_memory = (
        a.reshape(rows_here, tok_row, model_width) for a in leaving
    )
    return (
        output,
        grad_tokens,
        grad_memory,
        gain_grads[0],
        gain_grads[1],
        gain_grads[2],
        query_out,
        key_out,
        value_out,
        out_out,
        gate_out,
        up_out,
        down_out,
    )


def solution(mesh):
    dp, ulysses, blk = (mesh.shape[axis] for axis in ("dp", "ulysses", "blk"))
    mesh = jax.sharding.Mesh(mesh.devices.reshape(dp // 2, 2, 2, ulysses // 2, blk), AXES)
    dp, places = ("dh", "dl"), ("uh", "ul", "blk")
    rows = P(dp, places, None)
    weight = P(AXES, None)
    grad = P(dp, places)
    return jax.shard_map(
        on_device,
        mesh=mesh,
        in_specs=(rows, rows, P(dp, None), P(), P(), P()) + (weight,) * 7 + (rows,),
        out_specs=(rows,) * 3 + (P(AXES),) * 3 + (grad,) * 7,
        check_vma=False,
    )
```

```python
import functools

import jax
import jax.numpy as jnp
from jax import lax
from jax.experimental import pallas as pl
from jax.experimental.pallas import tpu as pltpu
from jax.sharding import PartitionSpec as P

H = 16
HD = 128
AXES = ("dh", "dl", "uh", "ul", "blk")
GROUP = ("dl", "ul", "blk")
INNER = ("ul", "blk")
bf16 = jnp.bfloat16
f32 = jnp.float32
epsilon = 1e-06
negative = -1e30


def dot(left, right, over, kind=f32):
    return lax.dot_general(left, right, (over, ((), ())), preferred_element_type=kind)


def times(left, right, kind=f32):
    return dot(left, right, ((1,), (0,)), kind)


def times_transposed(left, right, kind=f32):
    return dot(left, right, ((1,), (1,)), kind)


def transposed_times(left, right, kind=f32):
    return dot(left, right, ((0,), (0,)), kind)


def normalize(values):
    inverse = lax.rsqrt(jnp.mean(values * values, axis=-1, keepdims=True) + epsilon)
    return (values * inverse, inverse)


def norm_back(grad_normed, normed, inverse, gain):
    scaled = grad_normed * gain
    return inverse * (scaled - normed * jnp.mean(scaled * normed, axis=-1, keepdims=True))


def add_low(left, right):
    return (left.astype(f32) + right.astype(f32)).astype(bf16)


def masked_scores(q, k, start, place, key_place, scale):
    scores = times_transposed(q, k) * scale
    allowed = (key_place >= start) & (key_place <= place)
    return jnp.where(allowed, scores, negative)


def attention_parts(q_ref, kv_ref, okv_ref, info_ref, places_ref, scale):
    q = q_ref[0, :, 0].reshape(-1, HD)
    kv = kv_ref[0, :, 0].reshape(-1, 2 * HD)
    okv = okv_ref[0, :, 0].reshape(-1, 2 * HD)
    start = info_ref[0, 0, :, 0:1]
    place = info_ref[0, 0, :, 1:2]
    own = masked_scores(q, kv[:, :HD], start, place, places_ref[0:1, :], scale)
    other = masked_scores(q, okv[:, :HD], start, place, places_ref[1:2, :], scale)
    largest = jnp.maximum(
        jnp.max(own, axis=-1, keepdims=True), jnp.max(other, axis=-1, keepdims=True)
    )
    own = jnp.exp(own - largest)
    other = jnp.exp(other - largest)
    total = jnp.sum(own, axis=-1, keepdims=True) + jnp.sum(other, axis=-1, keepdims=True)
    return q, kv, okv, own / total, other / total


def attend_kernel(scale, q_ref, kv_ref, okv_ref, info_ref, places_ref, out_ref):
    _, kv, okv, own, other = attention_parts(q_ref, kv_ref, okv_ref, info_ref, places_ref, scale)
    mixed = times(own.astype(bf16), kv[:, HD:]) + times(other.astype(bf16), okv[:, HD:])
    out_ref[0, :, 0] = mixed.astype(bf16).reshape(out_ref.shape[1], out_ref.shape[3], HD)


def attend_back_kernel(
    scale, q_ref, kv_ref, okv_ref, g_ref, info_ref, places_ref, gq_ref, gkv_ref, gokv_ref
):
    q, kv, okv, own, other = attention_parts(q_ref, kv_ref, okv_ref, info_ref, places_ref, scale)
    g = g_ref[0, :, 0].reshape(-1, HD)
    grad_own = times_transposed(g, kv[:, HD:])
    grad_other = times_transposed(g, okv[:, HD:])
    centre = jnp.sum(own * grad_own, axis=-1, keepdims=True) + jnp.sum(
        other * grad_other, axis=-1, keepdims=True
    )
    score_own = (own * (grad_own - centre)).astype(bf16)
    score_other = (other * (grad_other - centre)).astype(bf16)

    def put(ref, lanes, value):
        ref[0, :, 0, :, lanes] = value.astype(ref.dtype).reshape(ref.shape[1], ref.shape[3], HD)

    first, second = slice(0, HD), slice(HD, 2 * HD)
    put(gokv_ref, first, transposed_times(score_other, q) * scale)
    put(gokv_ref, second, transposed_times(other.astype(bf16), g))
    put(gkv_ref, first, transposed_times(score_own, q) * scale)
    put(gkv_ref, second, transposed_times(own.astype(bf16), g))
    put(gq_ref, first, (times(score_own, kv[:, :HD]) + times(score_other, okv[:, :HD])) * scale)


def attention_call(kernel, inputs, info, places, outputs):
    twins, pieces, rows, tok, width = inputs[0].shape
    heads = width // HD
    span = pieces * tok

    def block(array):
        return pl.BlockSpec(
            (1, pieces, 1, tok, array.shape[-1] // heads), lambda c, r, h: (c, 0, r, 0, h)
        )

    return pl.pallas_call(
        kernel,
        grid=(twins, rows, heads),
        in_specs=[block(a) for a in inputs]
        + [
            pl.BlockSpec((1, 1, span, 2), lambda c, r, h: (c, r, 0, 0)),
            pl.BlockSpec(places.shape, lambda c, r, h: (0, 0)),
        ],
        out_specs=[block(a) for a in outputs],
        out_shape=outputs,
        compiler_params=pltpu.CompilerParams(vmem_limit_bytes=48 * 1024 * 1024),
        cost_estimate=pl.CostEstimate(flops=1, bytes_accessed=1, transcendentals=0),
    )(*inputs, info, places)


def twins_kernel(sides_ref, kept_ref, given_ref, out_ref):
    out_ref[...] = add_low(kept_ref[...], given_ref[...])


def owner_kernel(unit, sides_ref, kept_ref, given_ref, twins_ref, *outs):
    mine = kept_ref[...].astype(f32) + given_ref[...].astype(f32)
    mine = jnp.where(sides_ref[0] == sides_ref[1], mine, twins_ref[...].astype(f32))
    if len(outs) == 1:
        outs[0][...] = mine
        return
    for i in range(mine.shape[1] // unit):
        j = i // 2 * unit
        outs[i % 2][:, j : j + unit] = mine[:, i * unit : (i + 1) * unit]


def halves_call(turned, kernel, sides, inputs, maps, outputs):
    rows = inputs[0].shape[1 if turned else 0] // 4

    def block(pick, array):
        if turned:
            return pl.BlockSpec((array.shape[0], rows), lambda i, s: (0, pick(i, s[0], s[1])))
        return pl.BlockSpec((rows, array.shape[1]), lambda i, s: (pick(i, s[0], s[1]), 0))

    return pl.pallas_call(
        kernel,
        grid_spec=pltpu.PrefetchScalarGridSpec(
            num_scalar_prefetch=1,
            grid=(2,),
            in_specs=[block(pick, a) for pick, a in zip(maps, inputs)],
            out_specs=[block(lambda i, z, t: i, a) for a in outputs],
        ),
        out_shape=outputs,
        cost_estimate=pl.CostEstimate(
            flops=0,
            bytes_accessed=sum(a.size * a.dtype.itemsize for a in [*inputs, *outputs]),
            transcendentals=0,
        ),
    )(sides, *inputs)


def split_kernel(unit, *refs):
    *sources, out = refs
    number = len(sources)
    for j in range(out.shape[0]):
        cols = out.shape[2] // number
        for i, source in enumerate(sources):
            for u in range(cols // unit):
                place = (u * number + i) * unit
                first = j * cols + u * unit
                out[j, :, place : place + unit] = source[:, first : first + unit]


def stack_kernel(*refs):
    *sources, out = refs
    rows, cols = sources[0].shape[0], out.shape[2]
    for i, source in enumerate(sources):
        for j in range(out.shape[0]):
            out[j, i * rows : (i + 1) * rows] = source[:, j * cols : (j + 1) * cols]


def turn_kernel(source, *outs):
    rows = source.shape[1] // len(outs)
    for i, out in enumerate(outs):
        blocks = source[:, i * rows : (i + 1) * rows]
        out[...] = blocks.reshape(-1, blocks.shape[-1]).T


def permuted(value, flags):
    low = value.shape[1] // 8
    blocks = [value[:, i * low : (i + 1) * low] for i in (0, 2, 1, 3, 4, 6, 5, 7)]
    for mask, flag in ((2, flags[0]), (4, flags[1])):
        blocks = [jnp.where(flag, blocks[j ^ mask], blocks[j]) for j in range(8)]
    return blocks


def restored(value, flags):
    low = value.shape[1] // 8
    blocks = [value[:, i * low : (i + 1) * low] for i in range(8)]
    for mask, flag in ((2, flags[0]), (4, flags[1])):
        blocks = [jnp.where(flag, blocks[j ^ mask], blocks[j]) for j in range(8)]
    return [blocks[i] for i in (0, 2, 1, 3, 4, 6, 5, 7)]


def move_kernel(how, me_ref, *refs):
    flags = [me_ref[0] == 1, me_ref[1] == 1]
    number = len(refs) // 2
    for source, target in zip(refs[:number], refs[number:]):
        low = source.shape[1] // 8
        for i, block in enumerate(how(source[...], flags)):
            target[:, i * low : (i + 1) * low] = block


def local_call(kernel, scalars, inputs, outputs):
    vmem = pl.BlockSpec(memory_space=pltpu.VMEM)
    size = sum(a.size * a.dtype.itemsize for a in [*inputs, *outputs])
    return pl.pallas_call(
        kernel,
        in_specs=[pl.BlockSpec(memory_space=pltpu.SMEM)] * len(scalars) + [vmem] * len(inputs),
        out_specs=[vmem] * len(outputs),
        out_shape=outputs,
        compiler_params=pltpu.CompilerParams(vmem_limit_bytes=48 * 1024 * 1024),
        cost_estimate=pl.CostEstimate(flops=0, bytes_accessed=size, transcendentals=0),
    )(*scalars, *inputs)


class Places:
    def __init__(self):
        self.count = lax.axis_size(AXES)
        self.me = lax.axis_index(AXES)
        self.group = lax.axis_size(GROUP)
        self.half_bit = self.group // 2
        self.twin_bit = self.group
        self.far_bit = 2 * self.group
        self.z = lax.axis_index("uh")
        self.x = lax.axis_index("dh")
        self.twin = lax.axis_index("dl")

    def swap(self, value, mask):
        return lax.ppermute(value, AXES, [(i, i ^ mask) for i in range(self.count)])

    def send(self, value, mask, chosen):
        return lax.ppermute(
            value, AXES, [(i, i ^ mask) for i in range(self.count) if chosen(i)]
        )


def after(value, *others):
    if not others:
        return value
    return lax.optimization_barrier((value, others))[0]


def near_weights(at, weights, unit, *others):
    rows, width = weights[0].shape
    number, cols = len(weights), width // at.group
    kernel = functools.partial(split_kernel, unit) if unit else stack_kernel
    shape = (at.group, rows, number * cols) if unit else (at.group, number * rows, cols)
    (blocks,) = local_call(kernel, [], weights, [jax.ShapeDtypeStruct(shape, bf16)])
    if others:
        blocks = after(blocks, *others)
    near = lax.all_to_all(blocks, GROUP, split_axis=0, concat_axis=0, tiled=True)
    if unit:
        return near.reshape(at.group * rows, number * cols)
    return local_call(
        turn_kernel,
        [],
        [near],
        [jax.ShapeDtypeStruct((cols, at.group * rows), bf16)] * number,
    )


def gather(at, value):
    return lax.all_gather(value, GROUP, axis=0, tiled=True)


def scatter(at, pairs, product=times_transposed, before=(), behind=()):
    def term(side):
        total = None
        for left, right in pairs:
            part = lax.dynamic_slice_in_dim(left, side * (left.shape[0] // 2), left.shape[0] // 2)
            part = product(part, right)
            total = part if total is None else total + part
        return total

    given = at.swap(term(1 - at.twin).astype(bf16), at.twin_bit)
    kept = (term(at.twin) + given.astype(f32)).astype(bf16)
    kept = kept.reshape(at.half_bit, -1, kept.shape[1])
    if before:
        kept = after(kept, *before)
    at.kept = kept
    kept = lax.all_to_all(kept, INNER, split_axis=0, concat_axis=0, tiled=True)
    if behind:
        kept = after(kept, *behind)
    return jnp.sum(kept.astype(f32), axis=0)


class Gradient:
    def __init__(self, at, pairs, turned=False):
        self.at, self.turned = at, turned
        cut = pairs[0][0].shape[1] // 2
        self.first = [(left[:, :cut], right) for left, right in pairs]
        self.there = self.product([(left[:, cut:], right) for left, right in pairs]).astype(bf16)
        self.given = at.swap(self.there, at.far_bit)

    def product(self, pairs):
        if self.turned:
            ((left, right),) = pairs
            return transposed_times(right, left)
        terms = [transposed_times(left, right) for left, right in pairs]
        return terms[0] if len(terms) == 1 else jnp.concatenate(terms, axis=1)

    def away(self, i):
        return (i // self.at.half_bit) % 2 != (i // self.at.twin_bit) % 2

    def across(self, *others):
        self.here = self.product(self.first)
        kept = (self.here + self.given.astype(f32)).astype(bf16)
        self.kept = after(kept, *others) if others else kept
        self.back = self.at.send(self.kept, self.at.half_bit, self.away)

    def call(self, kernel, inputs, maps, widths, kind):
        sides = jnp.stack([self.at.z, self.at.twin]).astype(jnp.int32)
        span = self.kept.shape[1 if self.turned else 0] // 2
        outs = [
            jax.ShapeDtypeStruct((width, span) if self.turned else (span, width), kind)
            for width in widths
        ]
        return halves_call(self.turned, kernel, sides, inputs, maps, outs)

    def to_twin(self):
        (twins,) = self.call(
            twins_kernel,
            [self.kept, self.back],
            [lambda i, z, t: 2 * i + 1 - t, lambda i, z, t: 2 * (1 - i) + 1 - t],
            [self.kept.shape[0 if self.turned else 1]],
            bf16,
        )
        self.twins = self.at.send(twins, self.at.twin_bit, lambda i: not self.away(i))

    def finish(self, unit=None):
        cols = self.kept.shape[0 if self.turned else 1]
        outs = self.call(
            functools.partial(owner_kernel, unit),
            [self.kept, self.back, self.twins],
            [
                lambda i, z, t: 2 * (i ^ z) + t,
                lambda i, z, t: 2 * (1 - (i ^ z)) + t,
                lambda i, z, t: i ^ z,
            ],
            [cols // 2, cols // 2] if unit else [cols],
            f32,
        )
        return [out.T if self.turned else out for out in outs]


def reduce_gains(at, terms):
    number, width = terms.shape
    terms = terms.reshape(number, 2, 2, 2, -1)
    terms = jnp.where(at.x == 1, terms[:, ::-1], terms)
    terms = jnp.where(at.z == 1, terms[:, :, ::-1], terms)
    terms = terms.transpose(0, 1, 3, 2, 4).reshape(number, at.count, -1).transpose(1, 0, 2)
    terms = lax.all_to_all(terms, AXES, split_axis=0, concat_axis=0, tiled=True)
    return jnp.sum(terms, axis=0)


def on_device(
    tokens,
    memory,
    lengths,
    gain_attn,
    gain_memory,
    gain_ffn,
    w_query,
    w_key,
    w_value,
    w_out,
    w_gate,
    w_up,
    w_down,
    cotangent,
):
    at = Places()
    rows_here, tok_row, model_width = tokens.shape
    count = rows_here * tok_row
    group = at.group
    half = group // 2
    head_width = w_query.shape[1]
    own_width = head_width // group
    width = max(own_width, HD)
    scale = HD ** (-0.5)

    bounds = jnp.cumsum(lengths, axis=1)
    twin_bounds = at.swap(bounds, at.twin_bit)
    first = at.twin == 0
    all_bounds = jnp.stack(
        [jnp.where(first, bounds, twin_bounds), jnp.where(first, twin_bounds, bounds)]
    )
    span = half * tok_row
    places = jnp.arange(span, dtype=jnp.int32)
    own_places = at.z * span + places
    other_places = (1 - at.z) * span + places
    passed = all_bounds[:, :, None, :] <= own_places[None, None, :, None]
    starts = jnp.max(jnp.where(passed, all_bounds[:, :, None, :], 0), axis=-1)
    info = jnp.stack([starts, jnp.broadcast_to(own_places, starts.shape)], axis=-1)
    key_places = jnp.stack([own_places, other_places])
    position = at.me % group
    here = position * tok_row + jnp.arange(tok_row, dtype=jnp.int32)
    valid = (here[None] < bounds[:, -1:]).astype(f32).reshape(count, 1)

    unit = min(own_width, HD)
    cache_near = near_weights(at, [w_key, w_value], unit)
    query_near = near_weights(at, [w_query, w_out], own_width, cache_near)
    sides = jnp.stack([at.z, at.x]).astype(jnp.int32)
    entry = [a.reshape(count, model_width) for a in (memory, tokens, cotangent)] + [
        gain.reshape(1, model_width) for gain in (gain_attn, gain_memory, gain_ffn)
    ]
    memory, tokens, cotangent, gain_attn, gain_memory, gain_ffn = local_call(
        functools.partial(move_kernel, permuted),
        [sides],
        entry,
        [jax.ShapeDtypeStruct(a.shape, a.dtype) for a in entry],
    )
    residual_in = tokens.astype(f32)
    token_normed, token_inverse = normalize(residual_in)
    token_in = (token_normed * gain_attn).astype(bf16)
    memory_normed, memory_inverse = normalize(memory.astype(f32))
    memory_in = (memory_normed * gain_memory).astype(bf16)
    grad_final = cotangent.astype(f32) * valid

    parts = HD // own_width if own_width < HD else 1

    def widen(value):
        if parts == 1:
            return value
        assert parts == lax.axis_size("blk")
        return lax.all_gather(value, "blk", axis=1, tiled=True)

    def narrow(value):
        if parts == 1:
            return value
        return lax.dynamic_slice_in_dim(
            value, lax.axis_index("blk") * own_width, own_width, axis=1
        )

    def heads(value):
        return value.reshape(2, half, rows_here, tok_row, -1)

    memory_all = gather(at, after(memory_in, cache_near))
    cache_half = at.swap(cache_near, at.half_bit)
    cache_far = at.swap(cache_near, at.far_bit)
    cache_far_half = at.swap(cache_half, at.far_bit)
    cache_w = jnp.concatenate([cache_near, cache_half, cache_far, cache_far_half], axis=0)
    memory_all = after(memory_all, cache_half, cache_far, info, )
    query_later = after(query_near, cache_half)
    query_half = at.swap(query_later, at.half_bit)
    query_far = at.swap(query_later, at.far_bit)
    token_all = gather(at, after(token_in, memory_all))
    memory_all = after(memory_all, cache_w)

    def first_half(i):
        return (i // at.half_bit) % 2 == 0

    def second_half(i):
        return not first_half(i)

    cache = times(memory_all, cache_w, bf16)
    if parts > 1:
        cache = jnp.concatenate(
            [widen(cache[:, :own_width]), widen(cache[:, own_width:])], axis=1
        )
    cache = heads(cache)
    other_cache = at.send(cache, at.half_bit, first_half)
    gathered_tokens = token_all
    token_all = after(token_all, other_cache)
    query_far_half = at.swap(after(query_half, cache), at.far_bit)
    query_parts = [query_near, query_half, query_far, query_far_half]
    query_w = jnp.concatenate([part[:, :own_width] for part in query_parts], axis=0)
    out_w = jnp.concatenate([part[:, own_width:] for part in query_parts], axis=0)
    queries = heads(widen(times(token_all, query_w, bf16)))
    gate_near, up_near, down_near = near_weights(
        at, [w_gate, w_up, w_down], None, cache
    )
    (mixed,) = attention_call(
        functools.partial(attend_kernel, scale),
        [after(queries, gate_near), cache, other_cache],
        info,
        key_places,
        [queries],
    )
    gate_far, up_far, down_far = (
        at.swap(near, at.far_bit) for near in (gate_near, up_near, down_near)
    )
    mixed = narrow(mixed.reshape(group * count, width))
    mixed = after(mixed, gate_far)
    gate_half = at.swap(after(gate_near, other_cache), at.half_bit)

    def whole(near, half_part, far_part, far_half_part):
        return jnp.concatenate([near, half_part, far_part, far_half_part], axis=1)

    up_half = at.swap(after(up_near, gate_half), at.half_bit)
    residual = residual_in + scatter(
        at, [(mixed, out_w)], times_transposed, (gate_half,), (up_half, up_far)
    )
    ffn_normed, ffn_inverse = normalize(residual)
    ffn_in = (ffn_normed * gain_ffn).astype(bf16)
    down_half = at.swap(after(down_near, up_half), at.half_bit)
    gate_w = whole(gate_near, gate_half, gate_far, at.swap(gate_half, at.far_bit))
    up_w = whole(up_near, up_half, up_far, at.swap(up_half, at.far_bit))
    ffn_all = after(gather(at, ffn_in), down_half, down_far, up_w)
    final_all = gather(at, after(grad_final.astype(bf16), other_cache))
    gate = times_transposed(ffn_all, gate_w)
    up = times_transposed(ffn_all, after(up_w, gate))
    down_w = whole(
        down_near, after(down_half, up), down_far, at.swap(down_half, at.far_bit)
    )
    grad_hidden = times_transposed(final_all, down_w)
    gate_sigmoid = jax.nn.sigmoid(gate)
    silu = gate * gate_sigmoid
    hidden = (silu * up).astype(bf16)
    grad_gate_in = (
        grad_hidden * up * gate_sigmoid * (1.0 + gate * (1.0 - gate_sigmoid))
    ).astype(bf16)
    grad_up_in = (grad_hidden * silu).astype(bf16)
    gate_grad = Gradient(at, [(ffn_all, grad_gate_in)], True)
    up_grad = Gradient(at, [(ffn_all, grad_up_in)], True)
    grad_ffn_in = scatter(
        at,
        [(after(grad_gate_in, gate_grad.there, ), gate_w), (grad_up_in, up_w)],
        times,
        (),
        (),
    )
    grad_residual = grad_final + norm_back(grad_ffn_in, ffn_normed, ffn_inverse, gain_ffn)
    gain_ffn_term = jnp.sum(grad_ffn_in * ffn_normed, axis=0)
    grad_branch = grad_residual.astype(bf16)
    hidden = after(hidden, grad_branch)
    down_grad = Gradient(at, [(final_all, hidden)], True)
    branch_all = gather(at, after(grad_branch, gate_grad.given))
    gate_grad.across(grad_branch)
    up_grad.across()
    gathered = branch_all
    branch_all = after(branch_all, gate_grad.kept, up_grad.kept, )
    grad_mixed = heads(widen(times(branch_all, out_w, bf16)))
    grad_queries, grad_cache, grad_other_cache = attention_call(
        functools.partial(attend_back_kernel, scale),
        [queries, cache, other_cache, grad_mixed],
        info,
        key_places,
        [
            queries,
            jax.ShapeDtypeStruct(cache.shape, f32),
            cache,
        ],
    )
    given_cache = at.send(grad_other_cache, at.half_bit, second_half)
    grad_queries = narrow(grad_queries.reshape(group * count, width))
    output = residual + scatter(at, [(hidden, down_w)], times, (gathered,))
    gate_grad.to_twin()
    (gate_out,) = gate_grad.finish()
    query_grad = Gradient(at, [(token_all, grad_queries), (branch_all, mixed)])

    given_cache = after(
        given_cache,
        gate_out,


        query_grad.given,

    )
    up_grad.to_twin()
    grad_cache = (grad_cache + given_cache.astype(f32)).astype(bf16)
    grad_cache = grad_cache.reshape(group * count, 2 * width)
    if parts > 1:
        grad_cache = jnp.concatenate(
            [narrow(grad_cache[:, :width]), narrow(grad_cache[:, width:])], axis=1
        )
    cache_grad = Gradient(at, [(memory_all, grad_cache)])
    down_grad.across(grad_cache)
    cache_grad.across()
    grad_memory_in = scatter(
        at,
        [(after(grad_cache, cache_grad.there, down_grad.kept), cache_w)],
        times_transposed,
        (cache_grad.given, down_grad.back),
        (),
    )
    query_grad.across(cache_grad.kept, )
    down_grad.to_twin()
    (up_out,) = up_grad.finish()
    cache_grad.to_twin()
    grad_token_in = scatter(
        at,
        [(after(grad_queries, at.kept, cache_grad.kept), query_w)],
        times_transposed,
        (cache_grad.back,),
        (
            query_grad.back,
            cache_grad.twins,
            up_out,

        ),
    )

    cut = model_width // 2
    gain_memory_term = (
        jnp.concatenate(
            [
                jnp.sum(cache_grad.here * cache_w[:cut].astype(f32), axis=1),
                jnp.sum(cache_grad.there.astype(f32) * cache_w[cut:].astype(f32), axis=1),
            ]
        )
        / gain_memory[0]
    )
    gain_attn_term = jnp.sum(grad_token_in * token_normed, axis=0)
    gain_terms = jnp.stack([gain_attn_term, gain_memory_term, gain_ffn_term])
    gain_grads = reduce_gains(at, gain_terms)
    down_grad.twins = after(down_grad.twins, gain_terms)
    cache_grad.twins = after(cache_grad.twins, gain_terms)
    query_grad.back = query_grad.back

    grad_tokens = grad_residual + norm_back(grad_token_in, token_normed, token_inverse, gain_attn)
    grad_memory = norm_back(grad_memory_in, memory_normed, memory_inverse, gain_memory)
    leaving = [a.astype(bf16) for a in (output, grad_tokens, grad_memory)]
    leaving = local_call(
        functools.partial(move_kernel, restored),
        [sides],
        leaving,
        [jax.ShapeDtypeStruct(a.shape, a.dtype) for a in leaving],
    )
    query_grad.to_twin()
    (down_out,) = down_grad.finish()
    query_out, out_out = query_grad.finish(own_width)
    key_out, value_out = cache_grad.finish(unit)
    output, grad_tokens, grad_memory = (
        a.reshape(rows_here, tok_row, model_width) for a in leaving
    )
    return (
        output,
        grad_tokens,
        grad_memory,
        gain_grads[0],
        gain_grads[1],
        gain_grads[2],
        query_out,
        key_out,
        value_out,
        out_out,
        gate_out,
        up_out,
        down_out,
    )


def solution(mesh):
    dp, ulysses, blk = (mesh.shape[axis] for axis in ("dp", "ulysses", "blk"))
    mesh = jax.sharding.Mesh(mesh.devices.reshape(dp // 2, 2, 2, ulysses // 2, blk), AXES)
    dp, places = ("dh", "dl"), ("uh", "ul", "blk")
    rows = P(dp, places, None)
    weight = P(AXES, None)
    grad = P(dp, places)
    return jax.shard_map(
        on_device,
        mesh=mesh,
        in_specs=(rows, rows, P(dp, None), P(), P(), P()) + (weight,) * 7 + (rows,),
        out_specs=(rows,) * 3 + (P(AXES),) * 3 + (grad,) * 7,
        check_vma=False,
    )
```

```python
import functools

import jax
import jax.numpy as jnp
from jax import lax
from jax.experimental import pallas as pl
from jax.experimental.pallas import tpu as pltpu
from jax.sharding import PartitionSpec as P

H = 16
HD = 128
AXES = ("dh", "dl", "uh", "ul", "blk")
GROUP = ("dl", "ul", "blk")
INNER = ("ul", "blk")
bf16 = jnp.bfloat16
f32 = jnp.float32
epsilon = 1e-06
negative = -1e30


def dot(left, right, over, kind=f32):
    return lax.dot_general(left, right, (over, ((), ())), preferred_element_type=kind)


def times(left, right, kind=f32):
    return dot(left, right, ((1,), (0,)), kind)


def times_transposed(left, right, kind=f32):
    return dot(left, right, ((1,), (1,)), kind)


def transposed_times(left, right, kind=f32):
    return dot(left, right, ((0,), (0,)), kind)


def normalize(values):
    inverse = lax.rsqrt(jnp.mean(values * values, axis=-1, keepdims=True) + epsilon)
    return (values * inverse, inverse)


def norm_back(grad_normed, normed, inverse, gain):
    scaled = grad_normed * gain
    return inverse * (scaled - normed * jnp.mean(scaled * normed, axis=-1, keepdims=True))


def add_low(left, right):
    return (left.astype(f32) + right.astype(f32)).astype(bf16)


def masked_scores(q, k, start, place, key_place, scale):
    scores = times_transposed(q, k) * scale
    allowed = (key_place >= start) & (key_place <= place)
    return jnp.where(allowed, scores, negative)


def attention_parts(q_ref, kv_ref, okv_ref, info_ref, places_ref, scale):
    q = q_ref[0, :, 0].reshape(-1, HD)
    kv = kv_ref[0, :, 0].reshape(-1, 2 * HD)
    okv = okv_ref[0, :, 0].reshape(-1, 2 * HD)
    start = info_ref[0, 0, :, 0:1]
    place = info_ref[0, 0, :, 1:2]
    own = masked_scores(q, kv[:, :HD], start, place, places_ref[0:1, :], scale)
    other = masked_scores(q, okv[:, :HD], start, place, places_ref[1:2, :], scale)
    largest = jnp.maximum(
        jnp.max(own, axis=-1, keepdims=True), jnp.max(other, axis=-1, keepdims=True)
    )
    own = jnp.exp(own - largest)
    other = jnp.exp(other - largest)
    total = jnp.sum(own, axis=-1, keepdims=True) + jnp.sum(other, axis=-1, keepdims=True)
    return q, kv, okv, own / total, other / total


def attend_kernel(scale, q_ref, kv_ref, okv_ref, info_ref, places_ref, out_ref):
    _, kv, okv, own, other = attention_parts(q_ref, kv_ref, okv_ref, info_ref, places_ref, scale)
    mixed = times(own.astype(bf16), kv[:, HD:]) + times(other.astype(bf16), okv[:, HD:])
    out_ref[0, :, 0] = mixed.astype(bf16).reshape(out_ref.shape[1], out_ref.shape[3], HD)


def attend_back_kernel(
    scale, q_ref, kv_ref, okv_ref, g_ref, info_ref, places_ref, gq_ref, gkv_ref, gokv_ref
):
    q, kv, okv, own, other = attention_parts(q_ref, kv_ref, okv_ref, info_ref, places_ref, scale)
    g = g_ref[0, :, 0].reshape(-1, HD)
    grad_own = times_transposed(g, kv[:, HD:])
    grad_other = times_transposed(g, okv[:, HD:])
    centre = jnp.sum(own * grad_own, axis=-1, keepdims=True) + jnp.sum(
        other * grad_other, axis=-1, keepdims=True
    )
    score_own = (own * (grad_own - centre)).astype(bf16)
    score_other = (other * (grad_other - centre)).astype(bf16)

    def put(ref, lanes, value):
        ref[0, :, 0, :, lanes] = value.astype(ref.dtype).reshape(ref.shape[1], ref.shape[3], HD)

    first, second = slice(0, HD), slice(HD, 2 * HD)
    put(gokv_ref, first, transposed_times(score_other, q) * scale)
    put(gokv_ref, second, transposed_times(other.astype(bf16), g))
    put(gkv_ref, first, transposed_times(score_own, q) * scale)
    put(gkv_ref, second, transposed_times(own.astype(bf16), g))
    put(gq_ref, first, (times(score_own, kv[:, :HD]) + times(score_other, okv[:, :HD])) * scale)


def attention_call(kernel, inputs, info, places, outputs):
    twins, pieces, rows, tok, width = inputs[0].shape
    heads = width // HD
    span = pieces * tok

    def block(array):
        return pl.BlockSpec(
            (1, pieces, 1, tok, array.shape[-1] // heads), lambda c, r, h: (c, 0, r, 0, h)
        )

    return pl.pallas_call(
        kernel,
        grid=(twins, rows, heads),
        in_specs=[block(a) for a in inputs]
        + [
            pl.BlockSpec((1, 1, span, 2), lambda c, r, h: (c, r, 0, 0)),
            pl.BlockSpec(places.shape, lambda c, r, h: (0, 0)),
        ],
        out_specs=[block(a) for a in outputs],
        out_shape=outputs,
        compiler_params=pltpu.CompilerParams(vmem_limit_bytes=48 * 1024 * 1024),
        cost_estimate=pl.CostEstimate(flops=1, bytes_accessed=1, transcendentals=0),
    )(*inputs, info, places)


def twins_kernel(sides_ref, kept_ref, given_ref, out_ref):
    out_ref[...] = add_low(kept_ref[...], given_ref[...])


def owner_kernel(unit, sides_ref, kept_ref, given_ref, twins_ref, *outs):
    mine = kept_ref[...].astype(f32) + given_ref[...].astype(f32)
    mine = jnp.where(sides_ref[0] == sides_ref[1], mine, twins_ref[...].astype(f32))
    if len(outs) == 1:
        outs[0][...] = mine
        return
    for i in range(mine.shape[1] // unit):
        j = i // 2 * unit
        outs[i % 2][:, j : j + unit] = mine[:, i * unit : (i + 1) * unit]


def halves_call(turned, kernel, sides, inputs, maps, outputs):
    rows = inputs[0].shape[1 if turned else 0] // 4

    def block(pick, array):
        if turned:
            return pl.BlockSpec((array.shape[0], rows), lambda i, s: (0, pick(i, s[0], s[1])))
        return pl.BlockSpec((rows, array.shape[1]), lambda i, s: (pick(i, s[0], s[1]), 0))

    return pl.pallas_call(
        kernel,
        grid_spec=pltpu.PrefetchScalarGridSpec(
            num_scalar_prefetch=1,
            grid=(2,),
            in_specs=[block(pick, a) for pick, a in zip(maps, inputs)],
            out_specs=[block(lambda i, z, t: i, a) for a in outputs],
        ),
        out_shape=outputs,
        cost_estimate=pl.CostEstimate(
            flops=0,
            bytes_accessed=sum(a.size * a.dtype.itemsize for a in [*inputs, *outputs]),
            transcendentals=0,
        ),
    )(sides, *inputs)


def split_kernel(unit, *refs):
    *sources, out = refs
    number = len(sources)
    for j in range(out.shape[0]):
        cols = out.shape[2] // number
        for i, source in enumerate(sources):
            for u in range(cols // unit):
                place = (u * number + i) * unit
                first = j * cols + u * unit
                out[j, :, place : place + unit] = source[:, first : first + unit]


def stack_kernel(*refs):
    *sources, out = refs
    rows, cols = sources[0].shape[0], out.shape[2]
    for i, source in enumerate(sources):
        for j in range(out.shape[0]):
            out[j, i * rows : (i + 1) * rows] = source[:, j * cols : (j + 1) * cols]


def turn_kernel(source, *outs):
    rows = source.shape[1] // len(outs)
    for i, out in enumerate(outs):
        blocks = source[:, i * rows : (i + 1) * rows]
        out[...] = blocks.reshape(-1, blocks.shape[-1]).T


def permuted(value, flags):
    low = value.shape[1] // 8
    blocks = [value[:, i * low : (i + 1) * low] for i in (0, 2, 1, 3, 4, 6, 5, 7)]
    for mask, flag in ((2, flags[0]), (4, flags[1])):
        blocks = [jnp.where(flag, blocks[j ^ mask], blocks[j]) for j in range(8)]
    return blocks


def restored(value, flags):
    low = value.shape[1] // 8
    blocks = [value[:, i * low : (i + 1) * low] for i in range(8)]
    for mask, flag in ((2, flags[0]), (4, flags[1])):
        blocks = [jnp.where(flag, blocks[j ^ mask], blocks[j]) for j in range(8)]
    return [blocks[i] for i in (0, 2, 1, 3, 4, 6, 5, 7)]


def move_kernel(how, me_ref, *refs):
    flags = [me_ref[0] == 1, me_ref[1] == 1]
    number = len(refs) // 2
    for source, target in zip(refs[:number], refs[number:]):
        low = source.shape[1] // 8
        for i, block in enumerate(how(source[...], flags)):
            target[:, i * low : (i + 1) * low] = block


def local_call(kernel, scalars, inputs, outputs):
    vmem = pl.BlockSpec(memory_space=pltpu.VMEM)
    size = sum(a.size * a.dtype.itemsize for a in [*inputs, *outputs])
    return pl.pallas_call(
        kernel,
        in_specs=[pl.BlockSpec(memory_space=pltpu.SMEM)] * len(scalars) + [vmem] * len(inputs),
        out_specs=[vmem] * len(outputs),
        out_shape=outputs,
        compiler_params=pltpu.CompilerParams(vmem_limit_bytes=48 * 1024 * 1024),
        cost_estimate=pl.CostEstimate(flops=0, bytes_accessed=size, transcendentals=0),
    )(*scalars, *inputs)


class Places:
    def __init__(self):
        self.count = lax.axis_size(AXES)
        self.me = lax.axis_index(AXES)
        self.group = lax.axis_size(GROUP)
        self.half_bit = self.group // 2
        self.twin_bit = self.group
        self.far_bit = 2 * self.group
        self.z = lax.axis_index("uh")
        self.x = lax.axis_index("dh")
        self.twin = lax.axis_index("dl")

    def swap(self, value, mask):
        return lax.ppermute(value, AXES, [(i, i ^ mask) for i in range(self.count)])

    def send(self, value, mask, chosen):
        return lax.ppermute(
            value, AXES, [(i, i ^ mask) for i in range(self.count) if chosen(i)]
        )


def after(value, *others):
    if not others:
        return value
    return lax.optimization_barrier((value, others))[0]


def near_weights(at, weights, unit, *others):
    rows, width = weights[0].shape
    number, cols = len(weights), width // at.group
    kernel = functools.partial(split_kernel, unit) if unit else stack_kernel
    shape = (at.group, rows, number * cols) if unit else (at.group, number * rows, cols)
    (blocks,) = local_call(kernel, [], weights, [jax.ShapeDtypeStruct(shape, bf16)])
    if others:
        blocks = after(blocks, *others)
    near = lax.all_to_all(blocks, GROUP, split_axis=0, concat_axis=0, tiled=True)
    if unit:
        return near.reshape(at.group * rows, number * cols)
    return local_call(
        turn_kernel,
        [],
        [near],
        [jax.ShapeDtypeStruct((cols, at.group * rows), bf16)] * number,
    )


def gather(at, value):
    return lax.all_gather(value, GROUP, axis=0, tiled=True)


def scatter(at, pairs, product=times_transposed, before=(), behind=()):
    def term(side):
        total = None
        for left, right in pairs:
            part = lax.dynamic_slice_in_dim(left, side * (left.shape[0] // 2), left.shape[0] // 2)
            part = product(part, right)
            total = part if total is None else total + part
        return total

    given = at.swap(term(1 - at.twin).astype(bf16), at.twin_bit)
    kept = (term(at.twin) + given.astype(f32)).astype(bf16)
    kept = kept.reshape(at.half_bit, -1, kept.shape[1])
    if before:
        kept = after(kept, *before)
    at.kept = kept
    kept = lax.all_to_all(kept, INNER, split_axis=0, concat_axis=0, tiled=True)
    if behind:
        kept = after(kept, *behind)
    return jnp.sum(kept.astype(f32), axis=0)


class Gradient:
    def __init__(self, at, pairs, turned=False):
        self.at, self.turned = at, turned
        cut = pairs[0][0].shape[1] // 2
        self.first = [(left[:, :cut], right) for left, right in pairs]
        self.there = self.product([(left[:, cut:], right) for left, right in pairs]).astype(bf16)
        self.given = at.swap(self.there, at.far_bit)

    def product(self, pairs):
        if self.turned:
            ((left, right),) = pairs
            return transposed_times(right, left)
        terms = [transposed_times(left, right) for left, right in pairs]
        return terms[0] if len(terms) == 1 else jnp.concatenate(terms, axis=1)

    def away(self, i):
        return (i // self.at.half_bit) % 2 != (i // self.at.twin_bit) % 2

    def across(self, *others):
        self.here = self.product(self.first)
        kept = (self.here + self.given.astype(f32)).astype(bf16)
        self.kept = after(kept, *others) if others else kept
        self.back = self.at.send(self.kept, self.at.half_bit, self.away)

    def call(self, kernel, inputs, maps, widths, kind):
        sides = jnp.stack([self.at.z, self.at.twin]).astype(jnp.int32)
        span = self.kept.shape[1 if self.turned else 0] // 2
        outs = [
            jax.ShapeDtypeStruct((width, span) if self.turned else (span, width), kind)
            for width in widths
        ]
        return halves_call(self.turned, kernel, sides, inputs, maps, outs)

    def to_twin(self):
        (twins,) = self.call(
            twins_kernel,
            [self.kept, self.back],
            [lambda i, z, t: 2 * i + 1 - t, lambda i, z, t: 2 * (1 - i) + 1 - t],
            [self.kept.shape[0 if self.turned else 1]],
            bf16,
        )
        self.twins = self.at.send(twins, self.at.twin_bit, lambda i: not self.away(i))

    def finish(self, unit=None):
        cols = self.kept.shape[0 if self.turned else 1]
        outs = self.call(
            functools.partial(owner_kernel, unit),
            [self.kept, self.back, self.twins],
            [
                lambda i, z, t: 2 * (i ^ z) + t,
                lambda i, z, t: 2 * (1 - (i ^ z)) + t,
                lambda i, z, t: i ^ z,
            ],
            [cols // 2, cols // 2] if unit else [cols],
            f32,
        )
        return [out.T if self.turned else out for out in outs]


def reduce_gains(at, terms):
    number, width = terms.shape
    terms = terms.reshape(number, 2, 2, 2, -1)
    terms = jnp.where(at.x == 1, terms[:, ::-1], terms)
    terms = jnp.where(at.z == 1, terms[:, :, ::-1], terms)
    terms = terms.transpose(0, 1, 3, 2, 4).reshape(number, at.count, -1).transpose(1, 0, 2)
    terms = lax.all_to_all(terms, AXES, split_axis=0, concat_axis=0, tiled=True)
    return jnp.sum(terms, axis=0)


def on_device(
    tokens,
    memory,
    lengths,
    gain_attn,
    gain_memory,
    gain_ffn,
    w_query,
    w_key,
    w_value,
    w_out,
    w_gate,
    w_up,
    w_down,
    cotangent,
):
    at = Places()
    rows_here, tok_row, model_width = tokens.shape
    count = rows_here * tok_row
    group = at.group
    half = group // 2
    head_width = w_query.shape[1]
    own_width = head_width // group
    width = max(own_width, HD)
    scale = HD ** (-0.5)

    bounds = jnp.cumsum(lengths, axis=1)
    twin_bounds = at.swap(bounds, at.twin_bit)
    first = at.twin == 0
    all_bounds = jnp.stack(
        [jnp.where(first, bounds, twin_bounds), jnp.where(first, twin_bounds, bounds)]
    )
    span = half * tok_row
    places = jnp.arange(span, dtype=jnp.int32)
    own_places = at.z * span + places
    other_places = (1 - at.z) * span + places
    passed = all_bounds[:, :, None, :] <= own_places[None, None, :, None]
    starts = jnp.max(jnp.where(passed, all_bounds[:, :, None, :], 0), axis=-1)
    info = jnp.stack([starts, jnp.broadcast_to(own_places, starts.shape)], axis=-1)
    key_places = jnp.stack([own_places, other_places])
    position = at.me % group
    here = position * tok_row + jnp.arange(tok_row, dtype=jnp.int32)
    valid = (here[None] < bounds[:, -1:]).astype(f32).reshape(count, 1)

    unit = min(own_width, HD)
    cache_near = near_weights(at, [w_key, w_value], unit)
    query_near = near_weights(at, [w_query, w_out], own_width, cache_near)
    sides = jnp.stack([at.z, at.x]).astype(jnp.int32)
    entry = [a.reshape(count, model_width) for a in (memory, tokens, cotangent)] + [
        gain.reshape(1, model_width) for gain in (gain_attn, gain_memory, gain_ffn)
    ]
    memory, tokens, cotangent, gain_attn, gain_memory, gain_ffn = local_call(
        functools.partial(move_kernel, permuted),
        [sides],
        entry,
        [jax.ShapeDtypeStruct(a.shape, a.dtype) for a in entry],
    )
    residual_in = tokens.astype(f32)
    token_normed, token_inverse = normalize(residual_in)
    token_in = (token_normed * gain_attn).astype(bf16)
    memory_normed, memory_inverse = normalize(memory.astype(f32))
    memory_in = (memory_normed * gain_memory).astype(bf16)
    grad_final = cotangent.astype(f32) * valid

    parts = HD // own_width if own_width < HD else 1

    def widen(value):
        if parts == 1:
            return value
        assert parts == lax.axis_size("blk")
        return lax.all_gather(value, "blk", axis=1, tiled=True)

    def narrow(value):
        if parts == 1:
            return value
        return lax.dynamic_slice_in_dim(
            value, lax.axis_index("blk") * own_width, own_width, axis=1
        )

    def heads(value):
        return value.reshape(2, half, rows_here, tok_row, -1)

    memory_all = gather(at, after(memory_in, cache_near))
    cache_half = at.swap(cache_near, at.half_bit)
    cache_far = at.swap(cache_near, at.far_bit)
    cache_far_half = at.swap(cache_half, at.far_bit)
    cache_w = jnp.concatenate([cache_near, cache_half, cache_far, cache_far_half], axis=0)
    memory_all = after(memory_all, cache_half, cache_far, info, )
    query_later = after(query_near, cache_half)
    query_half = at.swap(query_later, at.half_bit)
    query_far = at.swap(query_later, at.far_bit)
    token_all = gather(at, after(token_in, memory_all))
    memory_all = after(memory_all, cache_w)

    def first_half(i):
        return (i // at.half_bit) % 2 == 0

    def second_half(i):
        return not first_half(i)

    cache = times(memory_all, cache_w, bf16)
    if parts > 1:
        cache = jnp.concatenate(
            [widen(cache[:, :own_width]), widen(cache[:, own_width:])], axis=1
        )
    cache = heads(cache)
    other_cache = at.send(cache, at.half_bit, first_half)
    gathered_tokens = token_all
    token_all = after(token_all, other_cache)
    query_far_half = at.swap(after(query_half, cache), at.far_bit)
    query_parts = [query_near, query_half, query_far, query_far_half]
    query_w = jnp.concatenate([part[:, :own_width] for part in query_parts], axis=0)
    out_w = jnp.concatenate([part[:, own_width:] for part in query_parts], axis=0)
    queries = heads(widen(times(token_all, query_w, bf16)))
    gate_near, up_near, down_near = near_weights(
        at, [w_gate, w_up, w_down], None, cache
    )
    (mixed,) = attention_call(
        functools.partial(attend_kernel, scale),
        [after(queries, gate_near), cache, other_cache],
        info,
        key_places,
        [queries],
    )
    gate_far, up_far, down_far = (
        at.swap(near, at.far_bit) for near in (gate_near, up_near, down_near)
    )
    mixed = narrow(mixed.reshape(group * count, width))
    mixed = after(mixed, gate_far)
    gate_half = at.swap(after(gate_near, other_cache), at.half_bit)

    def whole(near, half_part, far_part, far_half_part):
        return jnp.concatenate([near, half_part, far_part, far_half_part], axis=1)

    up_half = at.swap(after(up_near, gate_half), at.half_bit)
    residual = residual_in + scatter(
        at, [(mixed, out_w)], times_transposed, (gate_half,), (up_half, up_far)
    )
    ffn_normed, ffn_inverse = normalize(residual)
    ffn_in = (ffn_normed * gain_ffn).astype(bf16)
    down_half = at.swap(after(down_near, up_half), at.half_bit)
    gate_w = whole(gate_near, gate_half, gate_far, at.swap(gate_half, at.far_bit))
    up_w = whole(up_near, up_half, up_far, at.swap(up_half, at.far_bit))
    ffn_all = after(gather(at, ffn_in), down_half, down_far, gate_w, up_w)
    final_all = gather(at, after(grad_final.astype(bf16), other_cache))
    gate = times_transposed(ffn_all, gate_w)
    up = times_transposed(ffn_all, after(up_w, gate))
    down_w = whole(
        down_near, after(down_half, up), down_far, at.swap(down_half, at.far_bit)
    )
    grad_hidden = times_transposed(final_all, down_w)
    gate_sigmoid = jax.nn.sigmoid(gate)
    silu = gate * gate_sigmoid
    hidden = (silu * up).astype(bf16)
    grad_gate_in = (
        grad_hidden * up * gate_sigmoid * (1.0 + gate * (1.0 - gate_sigmoid))
    ).astype(bf16)
    grad_up_in = (grad_hidden * silu).astype(bf16)
    gate_grad = Gradient(at, [(ffn_all, grad_gate_in)], True)
    up_grad = Gradient(at, [(ffn_all, grad_up_in)], True)
    grad_ffn_in = scatter(
        at,
        [(after(grad_gate_in, gate_grad.there, ), gate_w), (grad_up_in, up_w)],
        times,
        (),
        (),
    )
    grad_residual = grad_final + norm_back(grad_ffn_in, ffn_normed, ffn_inverse, gain_ffn)
    gain_ffn_term = jnp.sum(grad_ffn_in * ffn_normed, axis=0)
    grad_branch = grad_residual.astype(bf16)
    hidden = after(hidden, grad_branch)
    down_grad = Gradient(at, [(final_all, hidden)], True)
    branch_all = gather(at, after(grad_branch, gate_grad.given))
    gate_grad.across(grad_branch)
    up_grad.across()
    gathered = branch_all
    branch_all = after(branch_all, gate_grad.kept, up_grad.kept, )
    grad_mixed = heads(widen(times(branch_all, out_w, bf16)))
    grad_queries, grad_cache, grad_other_cache = attention_call(
        functools.partial(attend_back_kernel, scale),
        [queries, cache, other_cache, grad_mixed],
        info,
        key_places,
        [
            queries,
            jax.ShapeDtypeStruct(cache.shape, f32),
            cache,
        ],
    )
    given_cache = at.send(grad_other_cache, at.half_bit, second_half)
    grad_queries = narrow(grad_queries.reshape(group * count, width))
    output = residual + scatter(at, [(hidden, down_w)], times, (gathered,))
    gate_grad.to_twin()
    (gate_out,) = gate_grad.finish()
    query_grad = Gradient(at, [(token_all, grad_queries), (branch_all, mixed)])

    given_cache = after(
        given_cache,
        gate_out,


        query_grad.given,

    )
    up_grad.to_twin()
    grad_cache = (grad_cache + given_cache.astype(f32)).astype(bf16)
    grad_cache = grad_cache.reshape(group * count, 2 * width)
    if parts > 1:
        grad_cache = jnp.concatenate(
            [narrow(grad_cache[:, :width]), narrow(grad_cache[:, width:])], axis=1
        )
    cache_grad = Gradient(at, [(memory_all, grad_cache)])
    down_grad.across(grad_cache)
    cache_grad.across()
    grad_memory_in = scatter(
        at,
        [(after(grad_cache, cache_grad.there, down_grad.kept), cache_w)],
        times_transposed,
        (cache_grad.given, down_grad.back),
        (),
    )
    query_grad.across(cache_grad.kept, )
    down_grad.to_twin()
    (up_out,) = up_grad.finish()
    cache_grad.to_twin()
    grad_token_in = scatter(
        at,
        [(after(grad_queries, at.kept, cache_grad.kept), query_w)],
        times_transposed,
        (cache_grad.back,),
        (
            query_grad.back,
            cache_grad.twins,
            up_out,

        ),
    )

    cut = model_width // 2
    gain_memory_term = (
        jnp.concatenate(
            [
                jnp.sum(cache_grad.here * cache_w[:cut].astype(f32), axis=1),
                jnp.sum(cache_grad.there.astype(f32) * cache_w[cut:].astype(f32), axis=1),
            ]
        )
        / gain_memory[0]
    )
    gain_attn_term = jnp.sum(grad_token_in * token_normed, axis=0)
    gain_terms = jnp.stack([gain_attn_term, gain_memory_term, gain_ffn_term])
    gain_grads = reduce_gains(at, gain_terms)
    down_grad.twins = after(down_grad.twins, gain_terms)
    cache_grad.twins = after(cache_grad.twins, gain_terms)
    query_grad.back = query_grad.back

    grad_tokens = grad_residual + norm_back(grad_token_in, token_normed, token_inverse, gain_attn)
    grad_memory = norm_back(grad_memory_in, memory_normed, memory_inverse, gain_memory)
    leaving = [a.astype(bf16) for a in (output, grad_tokens, grad_memory)]
    leaving = local_call(
        functools.partial(move_kernel, restored),
        [sides],
        leaving,
        [jax.ShapeDtypeStruct(a.shape, a.dtype) for a in leaving],
    )
    query_grad.to_twin()
    (down_out,) = down_grad.finish()
    query_out, out_out = query_grad.finish(own_width)
    key_out, value_out = cache_grad.finish(unit)
    output, grad_tokens, grad_memory = (
        a.reshape(rows_here, tok_row, model_width) for a in leaving
    )
    return (
        output,
        grad_tokens,
        grad_memory,
        gain_grads[0],
        gain_grads[1],
        gain_grads[2],
        query_out,
        key_out,
        value_out,
        out_out,
        gate_out,
        up_out,
        down_out,
    )


def solution(mesh):
    dp, ulysses, blk = (mesh.shape[axis] for axis in ("dp", "ulysses", "blk"))
    mesh = jax.sharding.Mesh(mesh.devices.reshape(dp // 2, 2, 2, ulysses // 2, blk), AXES)
    dp, places = ("dh", "dl"), ("uh", "ul", "blk")
    rows = P(dp, places, None)
    weight = P(AXES, None)
    grad = P(dp, places)
    return jax.shard_map(
        on_device,
        mesh=mesh,
        in_specs=(rows, rows, P(dp, None), P(), P(), P()) + (weight,) * 7 + (rows,),
        out_specs=(rows,) * 3 + (P(AXES),) * 3 + (grad,) * 7,
        check_vma=False,
    )
```
